256 devices in a mesh: dp: 32 (over y, z), section: 8 (over x, core).
Axes of the slice: x: 4, y: 4, z: 8, core: 2. Of those that a mesh axis runs over, the one named last changes fastest.
Arguments:
- grad_rows: bfloat16 [131072, 1280], P(('dp', 'section')), may hold values from -24 to 24
- layer_input: bfloat16 [196608, 1280], P(('dp', 'section')), may hold values from -18 to 18
- saved_qkv: bfloat16 [196608, 1920], P(('dp', 'section')), may hold values from -30 to 30
- image_patches: int32 [32, 32], P('dp'), may hold values from 0 to 256, as said below
- image_owner: int32 [32, 32], P('dp'), may hold values from 0 to 7, as said below
- norm_gain: float32 [1280], replicated, may hold values from 0.1 to 1.9
- norm_bias: float32 [1280], replicated, may hold values from -3 to 3
- w_qkv: bfloat16 [1280, 1920], P('dp'), may hold values from -0.15625 to 0.15625
- w_out: bfloat16 [1280, 640], P('dp'), may hold values from -0.25 to 0.25
Outputs:
- layer_grad: bfloat16 [196608, 1280], P(('dp', 'section'))
- qkv_weight_grad: float32 [1280, 1920], P('dp')
- out_weight_grad: float32 [1280, 640], P('dp')
The draws below stay inside these ranges and needn't reach their ends.
Inputs may be any that keep to these rules, and one draw needn't show every extreme that they name: `image_patches`: each row lists one dp index's images in order; their counts, multiples of 128, fill that index's 8 devices with exactly 512 rows each, in section order; an image may run on from the last tile of one device to the first tile of the next; after the last image the entries are 0. `image_owner`: the images of one owner in one row hold at most 768 rows together, exactly 768 for some owner of every row; each device hands at most 128 rows to one owner; entries after the last image are 0.
All inputs are finite; a program needn't handle non-finite values.
Results may differ from the reference program's by a relative error of at most 0.019.
Values may be sent and summed in bfloat16 or wider, within the bound.
No kernel may reach another device: no remote copies, remote signals or barrier semaphores. Data moves between devices by JAX's collectives and lax.ppermute only.
A program may use at most 192 MiB of HBM per device.

```python
import math
import jax
import jax.numpy as jnp
from jax import lax

D = 1280
HEADS = 8
HEAD_DIM = 80
TILE = 128
SRC_TILES = 4
OWN_TILES = 6
HW = 640
QKV = 1920
OWN_ROWS = 768
SRC_ALL = 131072
OWN_ALL = 196608
N_DP = 32
N_SECTION = 8


def column_plan(column_key):
    key_order, key_join, key_pick = jax.random.split(column_key, 3)
    sections = N_SECTION
    ordering = jax.random.permutation(key_order, sections).astype(jnp.int32)
    offsets = jnp.array([0, 2, 3, 1], dtype=jnp.int32)
    section_list = jnp.arange(sections, dtype=jnp.int32)
    owner_grid = ordering[(section_list[:, None] + offsets[None, :]) % sections]
    if sections >= 8:
        target = jax.random.randint(key_pick, (), 0, sections).astype(jnp.int32)
        first_row = (target - sections // 2) % sections
        second_row = (target - sections // 2 - 1) % sections
        moved_row = (section_list == first_row) | (section_list == second_row)
        column_one = jnp.arange(4, dtype=jnp.int32) == 1
        owner_grid = jnp.where(moved_row[:, None] & column_one[None, :], ordering[target], owner_grid)
    join_flags = jax.random.randint(key_join, (sections,), 0, 2).astype(jnp.int32)
    join_flags = join_flags.at[0].set(1).at[sections - 1].set(0)
    tile_owner = owner_grid.reshape(-1)
    position = jnp.arange(4 * sections, dtype=jnp.int32)
    device_of = position // 4
    slot_of = position % 4
    starts_join = (slot_of == 3) & (join_flags[device_of] == 1)
    previous = jnp.maximum(device_of - 1, 0)
    continues = (slot_of == 0) & (device_of > 0) & (join_flags[previous] == 1)
    image_sizes = jnp.where(continues, 0, jnp.where(starts_join, 2, 1)).astype(jnp.int32)
    sort_keys = jnp.where(image_sizes > 0, position, position + image_sizes.shape[0])
    moved = jnp.argsort(sort_keys, stable=True)
    image_sizes = image_sizes[moved]
    owner_each = jnp.where(image_sizes > 0, tile_owner[moved], 0)
    return ((image_sizes * TILE).astype(jnp.int32), owner_each.astype(jnp.int32))


def route_all(key):
    column_keys = jax.random.split(key, N_DP)
    return jax.vmap(column_plan)(column_keys)


def draw_image_patches(key, part):
    image_sizes, owner_each = route_all(key)
    return image_sizes


def draw_image_owner(key, part):
    image_sizes, owner_each = route_all(key)
    return owner_each


def draw_layer_input(key, part):
    key = jax.random.fold_in(key, 3)
    key_scale, key_shift, key_base = jax.random.split(key, 3)
    row_scale = jnp.exp(jax.random.uniform(key_scale, (OWN_ALL, 1), minval=math.log(0.25), maxval=math.log(4.0)))
    row_shift = jnp.clip(0.5 * jax.random.normal(key_shift, (OWN_ALL, 1)), -1.5, 1.5)
    base_draw = jnp.clip(jax.random.normal(key_base, (OWN_ALL, D)), -4.0, 4.0)
    return (row_scale * base_draw + row_shift).astype(jnp.float32).astype(jnp.bfloat16)


def draw_saved_qkv(key, part):
    key = jax.random.fold_in(key, 5)
    key_base = jax.random.fold_in(key, 0)
    base_draw = jnp.clip(jax.random.normal(key_base, (OWN_ALL, QKV)), -6.0, 6.0)
    return base_draw.astype(jnp.float32).astype(jnp.bfloat16)


def strengthened(values, rng, source, target, shards_of, factor):
    owner, partner = [(jnp.arange(values.shape[dim]) // (values.shape[dim] // shards_of)).reshape([-1 if axis == dim else 1 for axis in range(values.ndim)]) for dim in (source, target)]
    chosen = jax.random.permutation(rng, shards_of)[partner]
    strong = (owner == chosen) | (owner == (partner + shards_of // 2) % shards_of)
    return jnp.where(strong, factor * values, values)


def shard_levels(rng, dims, pieces, smallest, top_value):
    loudness, own = 1.0, jax.random.fold_in(rng, 6)
    for axis_at, shards_of in pieces:
        steps = jnp.exp(jax.random.uniform(jax.random.fold_in(own, axis_at), (shards_of,), jnp.float32, smallest / len(pieces), top_value / len(pieces)))
        loudness = loudness * jnp.repeat(steps, dims[axis_at] // shards_of).reshape([-1 if axis == axis_at else 1 for axis in range(len(dims))])
    return loudness


def gaussian(key, dims, deviation, bound, cuts=(), kind=jnp.bfloat16):
    result = jax.random.normal(key, dims, jnp.float32) * deviation
    if len(cuts) > 0:
        result = shard_levels(key, dims, cuts, -0.22, 0.18) * result
    return jnp.clip(result, min=-bound, max=bound).astype(kind)


def bell_draw_with(rng, shape, scale, most, shards, heavy, kind=jnp.bfloat16):
    entries = scale * jax.random.normal(rng, shape, jnp.float32)
    if shards:
        entries = entries * shard_levels(rng, shape, shards, -0.22, 0.18)
    return jnp.clip(strengthened(entries, jax.random.fold_in(rng, 3), *heavy), -most, most).astype(kind)


def setup_inputs(seed: int = 0) -> dict:
    keys = jax.random.split(jax.random.key(seed), 10)
    grad_rows = bell_draw_with(keys[0], (SRC_ALL, D), 1.0, 24.0, ((0, 256),), (0, 1, 256, 6.0))
    layer_input = draw_layer_input(jax.random.fold_in(keys[9], 71), 0)
    saved_qkv = draw_saved_qkv(jax.random.fold_in(keys[9], 71), 0)
    image_patches = draw_image_patches(jax.random.fold_in(keys[9], 71), 0)
    image_owner = draw_image_owner(jax.random.fold_in(keys[9], 71), 0)
    norm_gain = jnp.clip(1.0 + 0.18 * jax.random.normal(keys[5], (D,), jnp.float32), 0.1, 1.9)
    norm_bias = gaussian(keys[6], (D,), 0.5, 3.0, (), jnp.float32)
    w_qkv = gaussian(keys[7], (D, QKV), D ** -0.5, 0.15625, ((0, 32),))
    w_out = gaussian(keys[8], (D, HW), HW ** -0.5, 0.25, ((0, 32),))
    return {"grad_rows": grad_rows, "layer_input": layer_input, "saved_qkv": saved_qkv, "image_patches": image_patches, "image_owner": image_owner, "norm_gain": norm_gain, "norm_bias": norm_bias, "w_qkv": w_qkv, "w_out": w_out}


norm_eps = 1e-06

def route_column(patches, owners):
    image_count = patches.shape[0]
    tile_counts = (patches // TILE).astype(jnp.int32)
    index_list = jnp.arange(image_count, dtype=jnp.int32)
    earlier = index_list[:, None] > index_list[None, :]
    begins = lax.optimization_barrier(jnp.sum(jnp.where(earlier, tile_counts[None, :], 0), axis=1)).astype(jnp.int32)
    same_owner = owners[:, None] == owners[None, :]
    slot_start = lax.optimization_barrier(jnp.sum(jnp.where(earlier & same_owner, tile_counts[None, :], 0), axis=1)).astype(jnp.int32)
    return (tile_counts, begins, slot_start)

def tile_targets(tile_counts, begins, slot_start, owners, tile_total):
    position = jnp.arange(tile_total, dtype=jnp.int32)
    ends = begins + tile_counts
    image_of = lax.optimization_barrier(jnp.sum((ends[None, :] <= position[:, None]).astype(jnp.int32), axis=1)).astype(jnp.int32)
    chosen = image_of[:, None] == jnp.arange(tile_counts.shape[0], dtype=jnp.int32)[None, :]
    tile_owner = lax.optimization_barrier(jnp.sum(jnp.where(chosen, owners[None, :], 0), axis=1)).astype(jnp.int32)
    tile_slot = (lax.optimization_barrier(jnp.sum(jnp.where(chosen, (slot_start - begins)[None, :], 0), axis=1)) + position).astype(jnp.int32)
    return (tile_owner, tile_slot)

def owner_segments(tile_counts, slot_start, owners, section_index, own_tiles):
    image_count = tile_counts.shape[0]
    slot_grid = jnp.arange(own_tiles, dtype=jnp.int32)[:, None]
    covered = (owners[None, :] == section_index) & (slot_start[None, :] <= slot_grid) & (slot_grid < (slot_start + tile_counts)[None, :])
    image_id = lax.optimization_barrier(jnp.sum(jnp.where(covered, jnp.arange(image_count, dtype=jnp.int32)[None, :], 0), axis=1)).astype(jnp.int32)
    return jnp.where(jnp.any(covered, axis=1), image_id, -1).astype(jnp.int32)

def attend(qkv, segment):
    row_count = qkv.shape[0]
    heads = qkv.astype(jnp.float32).reshape(row_count, 3, HEADS, HEAD_DIM)
    score_scale = 1.0 / math.sqrt(HEAD_DIM)
    scores = jnp.einsum('rhd,shd->hrs', heads[:, 0], heads[:, 1]) * score_scale
    scores = jnp.where((segment[:, None] == segment[None, :])[None], scores, -jnp.inf)
    shifted = jnp.exp(scores - lax.optimization_barrier(jnp.max(scores, axis=2, keepdims=True)))
    probabilities = shifted / lax.optimization_barrier(jnp.sum(shifted, axis=2, keepdims=True))
    weights = probabilities.astype(jnp.bfloat16)
    attended = jnp.einsum('hrs,shd->rhd', weights.astype(jnp.float32), heads[:, 2])
    return (probabilities, weights, attended.astype(jnp.bfloat16).reshape(row_count, HEADS * HEAD_DIM))

def attend_back(qkv, probabilities, weights, attended, d_attn):
    row_count = qkv.shape[0]
    heads = qkv.astype(jnp.float32).reshape(row_count, 3, HEADS, HEAD_DIM)
    score_scale = 1.0 / math.sqrt(HEAD_DIM)
    grad_out = d_attn.astype(jnp.float32).reshape(row_count, HEADS, HEAD_DIM)
    row_delta = lax.optimization_barrier(jnp.sum(grad_out * attended.astype(jnp.float32).reshape(row_count, HEADS, HEAD_DIM), axis=2))
    prob_grad = jnp.einsum('rhd,shd->hrs', grad_out, heads[:, 2])
    dscore = (probabilities * (prob_grad - jnp.transpose(row_delta)[:, :, None]) * score_scale).astype(jnp.bfloat16)
    dscore_wide = dscore.astype(jnp.float32)
    dquery = jnp.einsum('hrs,shd->rhd', dscore_wide, heads[:, 1])
    key_grad = jnp.einsum('hrs,rhd->shd', dscore_wide, heads[:, 0])
    dvalues = jnp.einsum('hrs,rhd->shd', weights.astype(jnp.float32), grad_out)
    return jnp.stack([dquery, key_grad, dvalues], axis=1).reshape(row_count, 3 * HEADS * HEAD_DIM).astype(jnp.bfloat16)

def reference(grad_rows, layer_input, saved_qkv, image_patches, image_owner, norm_gain, norm_bias, w_qkv, w_out):
    sections = N_SECTION
    tile_total = sections * SRC_TILES

    def route_one(patches, owners):
        tile_counts, begins, slot_start = route_column(patches, owners)
        tile_owner, tile_slot = tile_targets(tile_counts, begins, slot_start, owners, tile_total)
        segments = jax.vmap(lambda section_index: owner_segments(tile_counts, slot_start, owners, section_index, OWN_TILES))(jnp.arange(sections, dtype=jnp.int32))
        return ((tile_owner * OWN_TILES + tile_slot).astype(jnp.int32), segments)
    targets, segments = jax.vmap(route_one)(image_patches, image_owner)
    tile_rows = grad_rows.reshape(N_DP, tile_total, TILE, D)

    def place_column(target_list, rows_here):
        empty_slots = jnp.zeros((sections * OWN_TILES, TILE, D), jnp.bfloat16)
        return empty_slots.at[target_list].set(rows_here)
    owned = jax.vmap(place_column)(targets, tile_rows).reshape(N_DP * sections, OWN_ROWS, D)
    segment_rows = jnp.repeat(segments.reshape(N_DP * sections, OWN_TILES), TILE, axis=1)
    inputs = layer_input.reshape(N_DP * sections, OWN_ROWS, D)
    qkv_blocks = saved_qkv.reshape(N_DP * sections, OWN_ROWS, QKV)

    def one_owner(running, owner_item):
        block_input, block_qkv, segment, incoming = owner_item
        widened = block_input.astype(jnp.float32)
        average = lax.optimization_barrier(jnp.mean(widened, axis=1, keepdims=True))
        centered = widened - average
        inv_scale = lax.rsqrt(lax.optimization_barrier(jnp.mean(centered * centered, axis=1, keepdims=True)) + norm_eps)
        normalized = centered * inv_scale
        normed = (normalized * norm_gain + norm_bias).astype(jnp.bfloat16)
        d_attn = jnp.dot(incoming, w_out, preferred_element_type=jnp.float32).astype(jnp.bfloat16)
        probabilities, weights, attended = attend(block_qkv, segment)
        dqkv = attend_back(block_qkv, probabilities, weights, attended, d_attn)
        dnormed = jnp.dot(dqkv, jnp.transpose(w_qkv), preferred_element_type=jnp.float32)
        scaled_grad = dnormed * norm_gain
        branch = inv_scale * (scaled_grad - lax.optimization_barrier(jnp.mean(scaled_grad, axis=1, keepdims=True)) - normalized * lax.optimization_barrier(jnp.mean(scaled_grad * normalized, axis=1, keepdims=True)))
        layer_grad = (incoming.astype(jnp.float32) + branch).astype(jnp.bfloat16)
        qkv_term = jnp.dot(jnp.transpose(normed), dqkv, preferred_element_type=jnp.float32)
        out_term = jnp.dot(jnp.transpose(incoming), attended, preferred_element_type=jnp.float32)
        return ((running[0] + qkv_term, running[1] + out_term), layer_grad)
    start_sums = (jnp.zeros((D, QKV), jnp.float32), jnp.zeros((D, HW), jnp.float32))
    sums, layer_grad = lax.scan(one_owner, start_sums, (inputs, qkv_blocks, segment_rows, owned))
    devices = N_DP * N_SECTION
    return (layer_grad.reshape(OWN_ALL, D), sums[0] / devices, sums[1] / devices)
```

```python
import functools
import math

import jax
import jax.numpy as jnp
from jax import lax
from jax.experimental import pallas as pl
from jax.experimental.pallas import tpu as pltpu
from jax.sharding import Mesh, PartitionSpec as P

HEADS = 8
HEAD_DIM = 80
TILE = 128
WINDOW = 2 * TILE
HW = HEADS * HEAD_DIM
SCALE = 1.0 / math.sqrt(HEAD_DIM)
BLOCKS = 4
AXES = {"y": 4, "z": 8, "x": 4, "core": 2}
VMEM_LIMIT = 56 * 1024 * 1024

norm_eps = 1e-06
f32 = jnp.float32
bf16 = jnp.bfloat16

SOURCE, START, JOINED, META = 0, 8, 16, 24


def lane_window(head):
    first, last = head * HEAD_DIM, (head + 1) * HEAD_DIM
    return first // 128 * 128, -(-last // 128) * 128


def params():
    return pltpu.CompilerParams(vmem_limit_bytes=VMEM_LIMIT)


def cost(flops, moved):
    return pl.CostEstimate(flops=flops, bytes_accessed=moved, transcendentals=0)


def route_kernel(patches, owners, place, rows, table, *rest, own_tiles, src_tiles, sections):
    outgoing = rest[:sections]
    used, segment, own_partner, sems = rest[sections:]
    me = place[0]
    for j in range(8):
        used[j] = 0
        segment[j] = -1
        table[SOURCE + j] = -1
    for j in range(src_tiles):
        own_partner[j] = 0

    def image(i, begin):
        count = patches[0, i] // TILE
        owner = owners[0, i]
        slot = used[owner]
        used[owner] = slot + count
        for t in range(2):

            @pl.when(t < count)
            def _():
                position = begin + t
                source = position // src_tiles

                @pl.when(owner == me)
                def _():
                    table[SOURCE + slot + t] = source ^ me
                    segment[slot + t] = i

                @pl.when(source == me)
                def _():
                    own_partner[position % src_tiles] = owner ^ me

        return begin + count

    lax.fori_loop(0, patches.shape[1], image, jnp.int32(0))
    copies = []
    for j in range(src_tiles):
        for k in range(sections):
            copy = pltpu.make_async_copy(rows.at[pl.ds(j * TILE, TILE)], outgoing[k], sems.at[j])
            pl.when(own_partner[j] == k)(copy.start)
        copies.append(copy)

    last = own_tiles - 1
    for b in range(8):
        table[START + b] = 0
        table[JOINED + b] = 0
        table[META + b] = 0
    table[META + 1] = place[1]
    at = jnp.int32(0)
    count = jnp.int32(0)
    lone = jnp.int32(0)

    def block(_, carry):
        at, count, lone = carry
        here = segment[at]
        after = segment[jnp.minimum(at + 1, last)]
        beyond = segment[jnp.minimum(at + 2, last)]
        joined = here == after
        splits = (at + 2 <= last) & (after == beyond) & jnp.logical_not(joined)
        active = at <= last
        is_lone = at == last

        @pl.when(active & jnp.logical_not(is_lone))
        def _():
            table[START + 1 + count] = at
            table[JOINED + 1 + count] = joined.astype(jnp.int32)

        @pl.when(is_lone)
        def _():
            table[START] = last - 1
            table[JOINED] = (segment[last - 1] == here).astype(jnp.int32)

        step = jnp.where(splits, 1, 2)
        return (
            jnp.where(active, at + step, at),
            count + jnp.where(active & jnp.logical_not(is_lone), 1, 0),
            lone | is_lone.astype(jnp.int32),
        )

    at, count, lone = lax.fori_loop(0, BLOCKS, block, (at, count, lone))
    table[META] = count
    table[META + 2] = lone
    for copy in copies:
        copy.wait()


def route(patches, owners, place, rows, own_tiles, sections):
    src_tiles = rows.shape[0] // TILE
    smem = pl.BlockSpec(memory_space=pltpu.SMEM)
    hbm = pl.BlockSpec(memory_space=pl.ANY)
    return pl.pallas_call(
        functools.partial(
            route_kernel, own_tiles=own_tiles, src_tiles=src_tiles, sections=sections
        ),
        out_shape=(
            jax.ShapeDtypeStruct((32,), jnp.int32),
            *(jax.ShapeDtypeStruct((TILE, rows.shape[1]), bf16) for _ in range(sections)),
        ),
        in_specs=[smem, smem, smem, pl.BlockSpec(memory_space=pltpu.VMEM)],
        out_specs=(smem, *(hbm for _ in range(sections))),
        scratch_shapes=[
            pltpu.SMEM((8,), jnp.int32),
            pltpu.SMEM((8,), jnp.int32),
            pltpu.SMEM((src_tiles,), jnp.int32),
            pltpu.SemaphoreType.DMA((src_tiles,)),
        ],
        compiler_params=params(),
        cost_estimate=cost(0, 4 * rows.size),
        name="route",
    )(patches, owners, place, rows)


def norm_kernel(x, gain, bias, out):
    wide = x[...].astype(f32)
    average = jnp.mean(wide, axis=1, keepdims=True)
    centered = wide - average
    inv_scale = lax.rsqrt(jnp.mean(centered * centered, axis=1, keepdims=True) + norm_eps)
    normed = centered * inv_scale * gain[...] + bias[...]
    out[...] = jnp.transpose(normed.astype(bf16))


def norm_transposed(x, gain, bias):
    rows, width = x.shape
    return pl.pallas_call(
        norm_kernel,
        grid=(rows // TILE,),
        out_shape=jax.ShapeDtypeStruct((width, rows), bf16),
        in_specs=[
            pl.BlockSpec((TILE, width), lambda t: (t, 0)),
            pl.BlockSpec((1, width), lambda t: (0, 0)),
            pl.BlockSpec((1, width), lambda t: (0, 0)),
        ],
        out_specs=pl.BlockSpec((width, TILE), lambda t: (0, t)),
        compiler_params=params(),
        cost_estimate=cost(20 * rows * width, 4 * rows * width),
        name="norm",
    )(x, gain.reshape(1, width), bias.reshape(1, width))


def padded_rows(values, head):
    low, high = lane_window(head)
    first = head * HEAD_DIM
    parts = []
    if first > low:
        parts.append(jnp.zeros((first - low, values.shape[1]), values.dtype))
    parts.append(values[first : first + HEAD_DIM])
    if high > first + HEAD_DIM:
        parts.append(jnp.zeros((high - first - HEAD_DIM, values.shape[1]), values.dtype))
    return jnp.concatenate(parts, axis=0) if len(parts) > 1 else parts[0]


def lane_mask(head):
    low, high = lane_window(head)
    lanes = lax.broadcasted_iota(jnp.int32, (1, high - low), 1) + low
    return ((lanes >= head * HEAD_DIM) & (lanes < (head + 1) * HEAD_DIM)).astype(f32).astype(bf16)


def matmul(a, b):
    return lax.dot_general(a, b, (((1,), (0,)), ((), ())), preferred_element_type=f32)


def block_is_used(table, b):
    return jnp.where(b == 0, table[META + 2], (b <= table[META]).astype(jnp.int32)) == 1


def forward_kernel(table, qkv, attended, attended_t, probabilities):
    b = pl.program_id(0)

    @pl.when(block_is_used(table, b))
    def _():
        start = pl.multiple_of(table[START + b] * TILE, TILE)
        rows = pl.ds(start, WINDOW)
        joined = table[JOINED + b] == 1
        key_tile = lax.broadcasted_iota(jnp.int32, (WINDOW, WINDOW), 0) // TILE
        query_tile = lax.broadcasted_iota(jnp.int32, (WINDOW, WINDOW), 1) // TILE
        kept = (key_tile == query_tile) | joined
        queries_t = jnp.transpose(qkv[rows, 0:HW])
        values_t = jnp.transpose(qkv[rows, 2 * HW : 3 * HW])
        heads = []
        for h in range(HEADS):
            low, high = lane_window(h)
            scores = matmul(qkv[rows, HW + low : HW + high], padded_rows(queries_t, h)) * SCALE
            scores = jnp.where(kept, scores, -jnp.inf)
            shifted = jnp.exp(scores - jnp.max(scores, axis=0, keepdims=True))
            probs = shifted * (1.0 / jnp.sum(shifted, axis=0, keepdims=True))
            probabilities[0, h] = probs
            heads.append(
                matmul(values_t[h * HEAD_DIM : (h + 1) * HEAD_DIM], probs.astype(bf16)).astype(bf16)
            )
        whole = jnp.concatenate(heads, axis=0)
        attended_t[0] = whole
        attended[rows, :] = jnp.transpose(whole)


def forward(table, qkv):
    rows, width = qkv.shape
    return pl.pallas_call(
        forward_kernel,
        grid_spec=pltpu.PrefetchScalarGridSpec(
            num_scalar_prefetch=1,
            grid=(BLOCKS + 1,),
            in_specs=[pl.BlockSpec((rows, width), lambda b, t: (0, 0))],
            out_specs=(
                pl.BlockSpec((rows, HW), lambda b, t: (0, 0)),
                pl.BlockSpec((1, HW, WINDOW), lambda b, t: (b, 0, 0)),
                pl.BlockSpec((1, HEADS, WINDOW, WINDOW), lambda b, t: (b, 0, 0, 0)),
            ),
        ),
        out_shape=(
            jax.ShapeDtypeStruct((rows, HW), bf16),
            jax.ShapeDtypeStruct((BLOCKS + 1, HW, WINDOW), bf16),
            jax.ShapeDtypeStruct((BLOCKS + 1, HEADS, WINDOW, WINDOW), f32),
        ),
        compiler_params=params(),
        cost_estimate=cost(8 * 10**9, 20 * 10**6),
        name="attend",
    )(table, qkv)


def incoming_kernel(table, own_w, mate_w, normed_t, *rest, sections, tiles):
    arrived = rest[:sections]
    incoming, d_attn, left_own, left_send, landing, sems = rest[sections:]
    t = pl.program_id(0)

    @pl.when(t == 0)
    def _():
        for j in range(tiles):
            for k in range(sections):
                copy = pltpu.make_async_copy(arrived[k], landing.at[j], sems.at[j])
                pl.when(table[SOURCE + j] == k)(copy.start)

    held = table[SOURCE + t] >= 0

    @pl.when(held)
    def _():
        pltpu.make_async_copy(arrived[0], landing.at[t], sems.at[t]).wait()

    rows = jnp.where(held, landing[t], jnp.zeros(landing.shape[1:], bf16))
    incoming[...] = rows
    rows_t = jnp.transpose(rows)
    first = table[META + 1] == 0
    left_own[...] = jnp.where(first, normed_t[...], rows_t)
    left_send[...] = jnp.where(first, rows_t, normed_t[...])

    @pl.when(first)
    def _():
        d_attn[:, 0:384] = matmul(rows, own_w[...]).astype(bf16)
        d_attn[:, 384:640] = matmul(rows, mate_w[:, 128:384]).astype(bf16)

    @pl.when(jnp.logical_not(first))
    def _():
        d_attn[:, 0:384] = matmul(rows, mate_w[...]).astype(bf16)
        d_attn[:, 384:640] = matmul(rows, own_w[:, 128:384]).astype(bf16)


def place_incoming(table, arrived, own_w, mate_w, normed_t):
    width, rows = normed_t.shape
    sections, tiles = len(arrived), rows // TILE
    tall = pl.BlockSpec((width, TILE), lambda i, t: (0, i))
    half = pl.BlockSpec((width, 384), lambda i, t: (0, 0))
    return pl.pallas_call(
        functools.partial(incoming_kernel, sections=sections, tiles=tiles),
        grid_spec=pltpu.PrefetchScalarGridSpec(
            num_scalar_prefetch=1,
            grid=(tiles,),
            in_specs=[half, half, tall] + [pl.BlockSpec(memory_space=pl.ANY)] * sections,
            out_specs=(
                pl.BlockSpec((TILE, width), lambda i, t: (i, 0)),
                pl.BlockSpec((TILE, HW), lambda i, t: (i, 0)),
                tall,
                tall,
            ),
            scratch_shapes=[
                pltpu.VMEM((tiles, TILE, width), bf16),
                pltpu.SemaphoreType.DMA((tiles,)),
            ],
        ),
        out_shape=(
            jax.ShapeDtypeStruct((rows, width), bf16),
            jax.ShapeDtypeStruct((rows, HW), bf16),
            jax.ShapeDtypeStruct((width, rows), bf16),
            jax.ShapeDtypeStruct((width, rows), bf16),
        ),
        compiler_params=params(),
        cost_estimate=cost(2 * rows * width * HW, 14 * rows * width),
        name="incoming",
    )(table, own_w, mate_w, normed_t, *arrived)


def backward_kernel(
    table,
    qkv,
    d_attn,
    attended,
    attended_t,
    probabilities,
    dqkv,
    first_own,
    first_send,
    second_own,
    second_send,
):
    b = pl.program_id(0)

    @pl.when(block_is_used(table, b))
    def _():
        start = pl.multiple_of(table[START + b] * TILE, TILE)
        rows = pl.ds(start, WINDOW)
        grad = d_attn[rows, :]
        grad_t = jnp.transpose(grad)
        keys_t = jnp.transpose(qkv[rows, HW : 2 * HW])
        query_grads = []
        key_tiles = [None] * (HW // 128)
        value_tiles = [None] * (HW // 128)

        def add(tiles, low, part):
            for j in range(part.shape[1] // 128):
                at = low // 128 + j
                piece = part[:, j * 128 : (j + 1) * 128]
                tiles[at] = piece if tiles[at] is None else tiles[at] + piece

        for h in range(HEADS):
            low, high = lane_window(h)
            mine = slice(h * HEAD_DIM, (h + 1) * HEAD_DIM)
            mask = lane_mask(h)
            probs = probabilities[0, h]
            prob_grad = matmul(qkv[rows, 2 * HW + low : 2 * HW + high], padded_rows(grad_t, h))
            row_delta = jnp.sum(
                grad_t[mine].astype(f32) * attended_t[0, mine].astype(f32), axis=0, keepdims=True
            )
            dscore = (probs * (prob_grad - row_delta) * SCALE).astype(bf16)
            query_grads.append(matmul(keys_t[mine], dscore).astype(bf16))
            add(key_tiles, low, matmul(dscore, qkv[rows, low:high] * mask))
            add(value_tiles, low, matmul(probs.astype(bf16), grad[:, low:high] * mask))
        dqkv[rows, 0:HW] = jnp.transpose(jnp.concatenate(query_grads, axis=0))
        for j in range(HW // 128):
            dqkv[rows, HW + j * 128 : HW + (j + 1) * 128] = key_tiles[j].astype(bf16)
            dqkv[rows, 2 * HW + j * 128 : 2 * HW + (j + 1) * 128] = value_tiles[j].astype(bf16)

    @pl.when(b == BLOCKS)
    def _():
        first = table[META + 1] == 0
        d_query, d_key, d_value = (dqkv[:, i * HW : (i + 1) * HW] for i in range(3))
        first_own[...] = jnp.where(first, d_value, attended[...])
        first_send[...] = jnp.where(first, attended[...], d_value)
        second_own[...] = jnp.where(first, d_query, d_key)
        second_send[...] = jnp.where(first, d_key, d_query)


def backward(table, qkv, d_attn, attended, attended_t, probabilities):
    rows, width = qkv.shape
    whole = pl.BlockSpec((rows, HW), lambda b, t: (0, 0))
    return pl.pallas_call(
        backward_kernel,
        grid_spec=pltpu.PrefetchScalarGridSpec(
            num_scalar_prefetch=1,
            grid=(BLOCKS + 1,),
            in_specs=[
                pl.BlockSpec((rows, width), lambda b, t: (0, 0)),
                whole,
                whole,
                pl.BlockSpec((1, HW, WINDOW), lambda b, t: (b, 0, 0)),
                pl.BlockSpec((1, HEADS, WINDOW, WINDOW), lambda b, t: (b, 0, 0, 0)),
            ],
            out_specs=(pl.BlockSpec((rows, width), lambda b, t: (0, 0)), whole, whole, whole, whole),
        ),
        out_shape=(
            jax.ShapeDtypeStruct((rows, width), bf16),
            *(jax.ShapeDtypeStruct((rows, HW), bf16) for _ in range(4)),
        ),
        compiler_params=params(),
        cost_estimate=cost(12 * 10**9, 25 * 10**6),
        name="attend_back",
    )(table, qkv, d_attn, attended, attended_t, probabilities)


def weight_kernel(left_own, left_mate, right_own, right_mate, out):
    total = matmul(left_own[...], right_own[...]) + matmul(left_mate[...], right_mate[...])
    rows = total.shape[0]
    group = rows // 4
    fifth = total[:, 512:640]
    quarter = lax.broadcasted_iota(jnp.int32, (group, 128), 1) // 32
    for x in range(4):
        packed = jnp.zeros((group, 128), f32)
        for g in range(4):
            piece = fifth[g * group : (g + 1) * group]
            shift = (g - x) * 32 % 128
            packed = jnp.where(quarter == g, pltpu.roll(piece, shift, 1) if shift else piece, packed)
        out[x, 0:rows] = total[:, x * 128 : (x + 1) * 128].astype(bf16)
        out[x, rows:] = packed.astype(bf16)


def weight_part(left_own, left_mate, right_own, right_mate, y_first):
    width, rows = left_own.shape
    piece = width // 4
    packed = piece * 5 // 4
    left = pl.BlockSpec((piece, rows), lambda i: (i, 0))
    right = pl.BlockSpec((rows, HW), lambda i: (0, 0))
    if y_first:
        out_spec = pl.BlockSpec((None, 4, packed, 128), lambda i: (i, 0, 0, 0))
    else:
        out_spec = pl.BlockSpec((4, None, packed, 128), lambda i: (0, i, 0, 0))
    return pl.pallas_call(
        weight_kernel,
        grid=(4,),
        out_shape=jax.ShapeDtypeStruct((4, 4, packed, 128), bf16),
        in_specs=[left, left, right, right],
        out_specs=out_spec,
        compiler_params=params(),
        cost_estimate=cost(4 * width * rows * HW, 4 * width * rows + 2 * width * HW),
        name="weight_part",
    )(left_own, left_mate, right_own, right_mate)


def unpacked(part):
    rest = part[320:]
    return jnp.concatenate(
        [part[:320], jnp.concatenate([rest[:, i * 32 : (i + 1) * 32] for i in range(4)], axis=0)], axis=1
    )


def to_mate(value):
    return lax.ppermute(value, "core", [(0, 1), (1, 0)])


def permuted_sum(value, axis):
    count = AXES[axis]
    here = lax.axis_index(axis)
    parts = [lax.dynamic_index_in_dim(value, here, 0, keepdims=False)]
    for k in range(1, count):
        part = lax.dynamic_index_in_dim(value, lax.rem(here + k, count), 0, keepdims=False)
        parts.append(lax.ppermute(part, axis, [(i, (i + k) % count) for i in range(count)]))
    return sum(part.astype(f32) for part in parts)


def exchanged(value, axes):
    return lax.all_to_all(value, axes, split_axis=0, concat_axis=0, tiled=True)


def on_device(
    grad_rows,
    layer_input,
    saved_qkv,
    image_patches,
    image_owner,
    norm_gain,
    norm_bias,
    w_qkv,
    w_out,
):
    width = layer_input.shape[1]
    own_tiles = layer_input.shape[0] // TILE
    section = ("x", "core")
    sections = AXES["x"] * AXES["core"]
    core = lax.axis_index("core")
    place = jnp.stack([lax.axis_index(section), core]).astype(jnp.int32)

    table, *outgoing = route(image_patches, image_owner, place, grad_rows, own_tiles, sections)
    all_w_qkv = lax.all_gather(w_qkv, ("y", "z"), axis=0, tiled=True)
    arrived = [outgoing[0]] + [
        lax.ppermute(outgoing[k], section, [(i, i ^ k) for i in range(sections)])
        for k in range(1, sections)
    ]
    w_out, _ = lax.optimization_barrier((w_out, table))
    half_w = lax.dynamic_slice_in_dim(w_out, 256 * core, 384, axis=1)
    half_w = exchanged(jnp.broadcast_to(half_w, (32,) + half_w.shape), ("y", "z"))
    half_w = half_w.reshape(width, 384)
    mate_w = to_mate(half_w)

    normed_t = norm_transposed(layer_input, norm_gain, norm_bias)
    mate_normed_t = to_mate(normed_t)
    attended, attended_t, probabilities = forward(table, saved_qkv)

    incoming, d_attn, left_own, left_send = place_incoming(table, arrived, half_w, mate_w, normed_t)
    left_mate = to_mate(left_send)
    dqkv, first_own, first_send, second_own, second_send = backward(
        table, saved_qkv, d_attn, attended, attended_t, probabilities
    )
    first_mate, second_mate = to_mate(first_send), to_mate(second_send)
    first = weight_part(left_own, left_mate, first_own, first_mate, True)
    second = weight_part(normed_t, mate_normed_t, second_own, second_mate, False)
    layer_grad = norm_back(layer_input, incoming, norm_gain, dqkv, all_w_qkv)

    first = jnp.sum(exchanged(first, "y").astype(f32), axis=0).astype(bf16)
    second = permuted_sum(second, "x").astype(bf16)
    first, second, layer_grad = lax.optimization_barrier((first, second, layer_grad))
    first = permuted_sum(first, "x")
    second = jnp.sum(exchanged(second, "y").astype(f32), axis=0)
    columns = jnp.concatenate([unpacked(first), unpacked(second)], axis=1)
    by_z = exchanged(columns.astype(bf16).reshape(8, 40, 320), "z")
    share = jnp.sum(by_z.astype(f32), axis=0) / (AXES["y"] * AXES["z"] * sections)
    shares = exchanged(jnp.broadcast_to(share, (sections,) + share.shape), section)

    def assemble(core, first_column):
        mine = [shares[2 * x + core][:, first_column : first_column + 160] for x in range(4)]
        return [part[:, :128] for part in mine] + [part[:, 128:] for part in mine]

    qkv_weight_grad = jnp.concatenate(assemble(0, 160) + assemble(1, 160) + assemble(0, 0), axis=1)
    out_weight_grad = jnp.concatenate(assemble(1, 0), axis=1)
    return layer_grad, qkv_weight_grad, out_weight_grad


def norm_back(layer_input, incoming, norm_gain, dqkv, w_qkv):
    widened = layer_input.astype(f32)
    average = jnp.mean(widened, axis=1, keepdims=True)
    centered = widened - average
    inv_scale = lax.rsqrt(jnp.mean(centered * centered, axis=1, keepdims=True) + norm_eps)
    normalized = centered * inv_scale
    dnormed = lax.dot_general(dqkv, w_qkv, (((1,), (1,)), ((), ())), preferred_element_type=f32)
    scaled_grad = dnormed * norm_gain
    branch = inv_scale * (
        scaled_grad
        - jnp.mean(scaled_grad, axis=1, keepdims=True)
        - normalized * jnp.mean(scaled_grad * normalized, axis=1, keepdims=True)
    )
    return (incoming.astype(f32) + branch).astype(bf16)


def solution(mesh):
    fine = Mesh(mesh.devices.reshape(tuple(AXES.values())), tuple(AXES))
    rows = P(("y", "z", "x", "core"), None)
    dp = P(("y", "z"), None)
    return jax.shard_map(
        on_device,
        mesh=fine,
        in_specs=(rows, rows, rows, dp, dp, P(), P(), dp, dp),
        out_specs=(rows, dp, dp),
        check_vma=False,
    )
```

```python
import functools
import math

import jax
import jax.numpy as jnp
from jax import lax
from jax.experimental import pallas as pl
from jax.experimental.pallas import tpu as pltpu
from jax.sharding import Mesh, PartitionSpec as P

HEADS = 8
HEAD_DIM = 80
TILE = 128
WINDOW = 2 * TILE
HW = HEADS * HEAD_DIM
SCALE = 1.0 / math.sqrt(HEAD_DIM)
BLOCKS = 4
AXES = {"y": 4, "z": 8, "x": 4, "core": 2}
VMEM_LIMIT = 60 * 1024 * 1024

norm_eps = 1e-06
f32 = jnp.float32
bf16 = jnp.bfloat16

SOURCE, START, JOINED, META = 0, 8, 16, 24


def lane_window(head):
    first, last = head * HEAD_DIM, (head + 1) * HEAD_DIM
    return first // 128 * 128, -(-last // 128) * 128


def params():
    return pltpu.CompilerParams(vmem_limit_bytes=VMEM_LIMIT)


def cost(flops, moved):
    return pl.CostEstimate(flops=flops, bytes_accessed=moved, transcendentals=0)


def route_kernel(
    patches, owners, place, rows, table, outgoing, used, segment, own_owner, sems, *, own_tiles, src_tiles
):
    me = place[0]
    for j in range(8):
        used[j] = 0
        segment[j] = -1
        table[SOURCE + j] = -1
    for j in range(src_tiles):
        own_owner[j] = 0

    def image(i, begin):
        count = patches[0, i] // TILE
        owner = owners[0, i]
        slot = used[owner]
        used[owner] = slot + count
        for t in range(2):

            @pl.when(t < count)
            def _():
                position = begin + t
                source = position // src_tiles

                @pl.when(owner == me)
                def _():
                    table[SOURCE + slot + t] = source
                    segment[slot + t] = i

                @pl.when(source == me)
                def _():
                    own_owner[position % src_tiles] = owner

        return begin + count

    lax.fori_loop(0, patches.shape[1], image, jnp.int32(0))
    copies = []
    for j in range(src_tiles):
        first_row = pl.multiple_of(own_owner[j] * TILE, TILE)
        copy = pltpu.make_async_copy(
            rows.at[pl.ds(j * TILE, TILE)], outgoing.at[pl.ds(first_row, TILE)], sems.at[j]
        )
        copy.start()
        copies.append(copy)

    last = own_tiles - 1
    for b in range(8):
        table[START + b] = 0
        table[JOINED + b] = 0
        table[META + b] = 0
    table[META + 1] = place[1]

    def step(at):
        here = segment[at]
        after = segment[jnp.minimum(at + 1, last)]
        beyond = segment[jnp.minimum(at + 2, last)]
        joined = here == after
        splits = (at + 2 <= last) & (after == beyond) & jnp.logical_not(joined)
        return at + jnp.where(splits, 1, 2), joined

    def find(_, carry):
        at, lone = carry
        moved, _ = step(jnp.minimum(at, last))
        return jnp.where(at <= last, moved, at), lone | (at == last).astype(jnp.int32)

    _, lone = lax.fori_loop(0, BLOCKS, find, (jnp.int32(0), jnp.int32(0)))

    @pl.when(lone == 1)
    def _():
        table[START] = last - 1
        table[JOINED] = (segment[last - 1] == segment[last]).astype(jnp.int32)

    def block(_, carry):
        at, count = carry
        moved, joined = step(jnp.minimum(at, last))
        active = at < last

        @pl.when(active)
        def _():
            table[START + count] = at
            table[JOINED + count] = joined.astype(jnp.int32)

        return jnp.where(active, moved, at), count + active.astype(jnp.int32)

    _, count = lax.fori_loop(0, BLOCKS, block, (jnp.int32(0), lone))
    table[META] = count
    for copy in copies:
        copy.wait()


def route(patches, owners, place, rows, own_tiles, sections):
    src_tiles = rows.shape[0] // TILE
    smem = pl.BlockSpec(memory_space=pltpu.SMEM)
    hbm = pl.BlockSpec(memory_space=pl.ANY)
    return pl.pallas_call(
        functools.partial(route_kernel, own_tiles=own_tiles, src_tiles=src_tiles),
        out_shape=(
            jax.ShapeDtypeStruct((32,), jnp.int32),
            jax.ShapeDtypeStruct((sections * TILE, rows.shape[1]), bf16),
        ),
        in_specs=[smem, smem, smem, pl.BlockSpec(memory_space=pltpu.VMEM)],
        out_specs=(smem, hbm),
        scratch_shapes=[
            pltpu.SMEM((8,), jnp.int32),
            pltpu.SMEM((8,), jnp.int32),
            pltpu.SMEM((src_tiles,), jnp.int32),
            pltpu.SemaphoreType.DMA((src_tiles,)),
        ],
        compiler_params=params(),
        cost_estimate=cost(0, 4 * rows.size),
        name="route",
    )(patches, owners, place, rows)


def norm_kernel(x, gain, bias, out):
    wide = x[...].astype(f32)
    average = jnp.mean(wide, axis=1, keepdims=True)
    centered = wide - average
    inv_scale = lax.rsqrt(jnp.mean(centered * centered, axis=1, keepdims=True) + norm_eps)
    normed = centered * inv_scale * gain[...] + bias[...]
    out[...] = jnp.transpose(normed.astype(bf16))


def norm_transposed(x, gain, bias):
    rows, width = x.shape
    return pl.pallas_call(
        norm_kernel,
        grid=(rows // TILE,),
        out_shape=jax.ShapeDtypeStruct((width, rows), bf16),
        in_specs=[
            pl.BlockSpec((TILE, width), lambda t: (t, 0)),
            pl.BlockSpec((1, width), lambda t: (0, 0)),
            pl.BlockSpec((1, width), lambda t: (0, 0)),
        ],
        out_specs=pl.BlockSpec((width, TILE), lambda t: (0, t)),
        compiler_params=params(),
        cost_estimate=cost(10**6, 10**5),
        name="norm",
    )(x, gain.reshape(1, width), bias.reshape(1, width))


def padded_rows(values, head):
    low, high = lane_window(head)
    first = head * HEAD_DIM
    parts = []
    if first > low:
        parts.append(jnp.zeros((first - low, values.shape[1]), values.dtype))
    parts.append(values[first : first + HEAD_DIM])
    if high > first + HEAD_DIM:
        parts.append(jnp.zeros((high - first - HEAD_DIM, values.shape[1]), values.dtype))
    return jnp.concatenate(parts, axis=0) if len(parts) > 1 else parts[0]


def lane_mask(head):
    low, high = lane_window(head)
    lanes = lax.broadcasted_iota(jnp.int32, (1, high - low), 1) + low
    return ((lanes >= head * HEAD_DIM) & (lanes < (head + 1) * HEAD_DIM)).astype(f32).astype(bf16)


def matmul(a, b):
    return lax.dot_general(a, b, (((1,), (0,)), ((), ())), preferred_element_type=f32)


def block_at(rank):
    return lambda b, t: (jnp.minimum(b, jnp.maximum(t[META] - 1, 0)),) + (0,) * (rank - 1)


def softmax_over_rows(scores):
    scores = scores * (SCALE * math.log2(math.e))
    shifted = jnp.exp2(scores - jnp.max(scores, axis=0, keepdims=True))
    return (shifted * (1.0 / jnp.sum(shifted, axis=0, keepdims=True))).astype(bf16)


def forward_kernel(table, qkv, attended, attended_t, weights):
    b = pl.program_id(0)
    rows = pl.ds(pl.multiple_of(table[START + b] * TILE, TILE), WINDOW)
    joined = table[JOINED + b] == 1

    def attend(whole_window):
        queries_t = jnp.transpose(qkv[rows, 0:HW])
        values_t = jnp.transpose(qkv[rows, 2 * HW : 3 * HW])

        def scores_of(h):
            low, high = lane_window(h)
            return matmul(qkv[rows, HW + low : HW + high], padded_rows(queries_t, h))

        heads = []
        for h in range(HEADS):
            scores = scores_of(h)
            if whole_window:
                kept = softmax_over_rows(scores)
            else:
                nothing = jnp.zeros((TILE, TILE), bf16)
                top = softmax_over_rows(scores[:TILE, :TILE])
                bottom = softmax_over_rows(scores[TILE:, TILE:])
                kept = jnp.concatenate(
                    [
                        jnp.concatenate([top, nothing], axis=1),
                        jnp.concatenate([nothing, bottom], axis=1),
                    ],
                    axis=0,
                )
            weights[0, h] = kept
            heads.append(matmul(values_t[h * HEAD_DIM : (h + 1) * HEAD_DIM], kept).astype(bf16))
        whole = jnp.concatenate(heads, axis=0)
        attended_t[0] = whole
        attended[rows, :] = jnp.transpose(whole)

    pl.when((b < table[META]) & joined)(lambda: attend(True))
    pl.when((b < table[META]) & jnp.logical_not(joined))(lambda: attend(False))


def forward(table, qkv):
    rows, width = qkv.shape
    return pl.pallas_call(
        forward_kernel,
        grid_spec=pltpu.PrefetchScalarGridSpec(
            num_scalar_prefetch=1,
            grid=(BLOCKS,),
            in_specs=[pl.BlockSpec((rows, width), lambda b, t: (0, 0))],
            out_specs=(
                pl.BlockSpec((rows, HW), lambda b, t: (0, 0)),
                pl.BlockSpec((1, HW, WINDOW), block_at(3)),
                pl.BlockSpec((1, HEADS, WINDOW, WINDOW), block_at(4)),
            ),
        ),
        out_shape=(
            jax.ShapeDtypeStruct((rows, HW), bf16),
            jax.ShapeDtypeStruct((BLOCKS, HW, WINDOW), bf16),
            jax.ShapeDtypeStruct((BLOCKS, HEADS, WINDOW, WINDOW), bf16),
        ),
        compiler_params=params(),
        cost_estimate=cost(10**6, 10**5),
        name="attend",
    )(table, qkv)


def incoming_kernel(table, arrived, w, incoming, d_attn, incoming_t, landing, sems, *, tiles):
    t = pl.program_id(0)

    def row_copy(j, source):
        first_row = pl.multiple_of(source * TILE, TILE)
        return pltpu.make_async_copy(
            arrived.at[pl.ds(first_row, TILE)], landing.at[pl.ds(j * TILE, TILE)], sems.at[j]
        )

    @pl.when(t == 0)
    def _():
        for j in range(tiles):
            source = table[SOURCE + j]

            @pl.when(source >= 0)
            def _():
                row_copy(j, source).start()

            @pl.when(source < 0)
            def _():
                landing[j * TILE : (j + 1) * TILE] = jnp.zeros((TILE, landing.shape[1]), bf16)

    for i in range(2):
        j = 2 * t + i
        pl.when(table[SOURCE + j] >= 0)(row_copy(j, 0).wait)
    rows = landing[pl.ds(pl.multiple_of(t * WINDOW, WINDOW), WINDOW)]
    incoming[...] = rows
    incoming_t[...] = jnp.transpose(rows)
    d_attn[...] = matmul(rows, w[...]).astype(bf16)


def place_incoming(table, arrived, w, rows):
    width = arrived.shape[1]
    return pl.pallas_call(
        functools.partial(incoming_kernel, tiles=rows // TILE),
        grid_spec=pltpu.PrefetchScalarGridSpec(
            num_scalar_prefetch=1,
            grid=(rows // WINDOW,),
            in_specs=[
                pl.BlockSpec(memory_space=pl.ANY),
                pl.BlockSpec((width, HW), lambda i, t: (0, 0)),
            ],
            out_specs=(
                pl.BlockSpec((WINDOW, width), lambda i, t: (i, 0)),
                pl.BlockSpec((WINDOW, HW), lambda i, t: (i, 0)),
                pl.BlockSpec((width, WINDOW), lambda i, t: (0, i)),
            ),
            scratch_shapes=[
                pltpu.VMEM((rows, width), bf16),
                pltpu.SemaphoreType.DMA((rows // TILE,)),
            ],
        ),
        out_shape=(
            jax.ShapeDtypeStruct((rows, width), bf16),
            jax.ShapeDtypeStruct((rows, HW), bf16),
            jax.ShapeDtypeStruct((width, rows), bf16),
        ),
        compiler_params=params(),
        cost_estimate=cost(2 * rows * width * HW, 10 * rows * width),
        name="incoming",
    )(table, arrived, w)


def add_lanes(tiles, low, part):
    for j in range(part.shape[1] // 128):
        piece = part[:, j * 128 : (j + 1) * 128]
        at = low // 128 + j
        tiles[at] = piece if tiles[at] is None else tiles[at] + piece


def backward_kernel(
    table, qkv, d_attn, attended, attended_t, weights, value_query, attended_key
):
    b = pl.program_id(0)

    @pl.when(b < table[META])
    def _():
        rows = pl.ds(pl.multiple_of(table[START + b] * TILE, TILE), WINDOW)
        grad_t = jnp.transpose(d_attn[rows, :])
        keys_t = jnp.transpose(qkv[rows, HW : 2 * HW])
        query_grads = []
        key_tiles = [None] * (HW // 128)
        value_tiles = [None] * (HW // 128)
        for h in range(HEADS):
            low, high = lane_window(h)
            mine = slice(h * HEAD_DIM, (h + 1) * HEAD_DIM)
            mask = lane_mask(h)
            prob_grad = matmul(qkv[rows, 2 * HW + low : 2 * HW + high], padded_rows(grad_t, h))
            row_delta = jnp.sum(
                grad_t[mine].astype(f32) * attended_t[0, mine].astype(f32), axis=0, keepdims=True
            )
            dscore = (weights[0, h].astype(f32) * ((prob_grad - row_delta) * SCALE)).astype(bf16)
            query_grads.append(matmul(keys_t[mine], dscore).astype(bf16))
            add_lanes(key_tiles, low, matmul(dscore, qkv[rows, low:high] * mask))
            add_lanes(value_tiles, low, matmul(weights[0, h], d_attn[rows, low:high] * mask))
        value_query[rows, HW:] = jnp.transpose(jnp.concatenate(query_grads, axis=0))
        for j in range(HW // 128):
            value_query[rows, j * 128 : (j + 1) * 128] = value_tiles[j].astype(bf16)
            attended_key[rows, HW + j * 128 : HW + (j + 1) * 128] = key_tiles[j].astype(bf16)
        attended_key[rows, :HW] = attended[rows, :]


def backward(table, qkv, d_attn, attended, attended_t, weights):
    rows, width = qkv.shape
    whole = pl.BlockSpec((rows, HW), lambda b, t: (0, 0))
    return pl.pallas_call(
        backward_kernel,
        grid_spec=pltpu.PrefetchScalarGridSpec(
            num_scalar_prefetch=1,
            grid=(BLOCKS,),
            in_specs=[
                pl.BlockSpec((rows, width), lambda b, t: (0, 0)),
                whole,
                whole,
                pl.BlockSpec((1, HW, WINDOW), block_at(3)),
                pl.BlockSpec((1, HEADS, WINDOW, WINDOW), block_at(4)),
            ],
            out_specs=(pl.BlockSpec((rows, 2 * HW), lambda b, t: (0, 0)),) * 2,
        ),
        out_shape=(jax.ShapeDtypeStruct((rows, 2 * HW), bf16),) * 2,
        compiler_params=params(),
        cost_estimate=cost(12 * 10**9, 20 * 10**6),
        name="attend_back",
    )(table, qkv, d_attn, attended, attended_t, weights)


def norm_back_kernel(table, x, incoming, gain, d_query, d_key, d_value, own_w, mate_w, out):
    def halves(low, high):
        grads = jnp.concatenate([d_query[...], d_key[...], d_value[...]], axis=1)
        contract = (((1,), (1,)), ((), ()))
        return lax.dot_general(
            grads[:, :1024], low[...], contract, preferred_element_type=f32
        ) + lax.dot_general(
            grads[:, 1024:], high[:, 128:1024], contract, preferred_element_type=f32
        )

    def finish(dnormed):
        wide = x[...].astype(f32)
        average = jnp.mean(wide, axis=1, keepdims=True)
        centered = wide - average
        inv_scale = lax.rsqrt(jnp.mean(centered * centered, axis=1, keepdims=True) + norm_eps)
        normalized = centered * inv_scale
        scaled_grad = dnormed * gain[...]
        branch = inv_scale * (
            scaled_grad
            - jnp.mean(scaled_grad, axis=1, keepdims=True)
            - normalized * jnp.mean(scaled_grad * normalized, axis=1, keepdims=True)
        )
        out[...] = (incoming[...].astype(f32) + branch).astype(bf16)

    first = table[META + 1] == 0

    @pl.when(first)
    def _():
        finish(halves(own_w, mate_w))

    @pl.when(jnp.logical_not(first))
    def _():
        finish(halves(mate_w, own_w))


def norm_back(table, x, incoming, gain, value_query, attended_key, own_w, mate_w):
    rows, width = x.shape
    wide = pl.BlockSpec((WINDOW, width), lambda i, t: (i, 0))
    weights = pl.BlockSpec((width, 1024), lambda i, t: (0, 0))
    return pl.pallas_call(
        norm_back_kernel,
        grid_spec=pltpu.PrefetchScalarGridSpec(
            num_scalar_prefetch=1,
            grid=(rows // WINDOW,),
            in_specs=[
                wide,
                wide,
                pl.BlockSpec((1, width), lambda i, t: (0, 0)),
                pl.BlockSpec((WINDOW, HW), lambda i, t: (i, 1)),
                pl.BlockSpec((WINDOW, HW), lambda i, t: (i, 1)),
                pl.BlockSpec((WINDOW, HW), lambda i, t: (i, 0)),
                weights,
                weights,
            ],
            out_specs=wide,
        ),
        out_shape=jax.ShapeDtypeStruct((rows, width), bf16),
        compiler_params=params(),
        cost_estimate=cost(2 * rows * width * 3 * HW, 20 * 10**6),
        name="norm_back",
    )(table, x, incoming, gain.reshape(1, width), value_query, attended_key, value_query, own_w, mate_w)


def packed_columns(total, out):
    rows = total.shape[0]
    group = rows // 4
    fifth = total[:, 512:640]
    quarter = lax.broadcasted_iota(jnp.int32, (group, 128), 1) // 32
    for x in range(4):
        packed = jnp.zeros((group, 128), f32)
        for g in range(4):
            piece = fifth[g * group : (g + 1) * group]
            shift = (g - x) * 32 % 128
            packed = jnp.where(quarter == g, pltpu.roll(piece, shift, 1) if shift else piece, packed)
        out[x, :rows] = total[:, x * 128 : (x + 1) * 128].astype(bf16)
        out[x, rows:] = packed.astype(bf16)


def weight_kernel(
    table, normed, mate_normed, incoming, mate_incoming, zero, one, mate_zero, mate_one, by_y, by_x, right, sems
):
    first = table[META + 1] == 0
    depth = zero.shape[0]

    def copy(side, source):
        return pltpu.make_async_copy(source, right.at[pl.ds(side * depth, depth)], sems.at[side])

    @pl.when(pl.program_id(0) == 0)
    def _():
        for side, (on_zero, on_one) in enumerate(((zero, one), (mate_zero, mate_one))):
            pl.when(first)(copy(side, on_zero).start)
            pl.when(jnp.logical_not(first))(copy(side, on_one).start)
        for side in range(2):
            copy(side, zero).wait()

    normed_both = jnp.concatenate([normed[...], mate_normed[...]], axis=1)
    incoming_both = jnp.concatenate([incoming[...], mate_incoming[...]], axis=1)
    left = jnp.where(first, normed_both, incoming_both)
    packed_columns(matmul(left, right[:, :HW]), by_y)
    packed_columns(matmul(normed_both, right[:, HW:]), by_x)


def weight_parts(table, normed, mate_normed, incoming, mate_incoming, rights):
    width, rows = normed.shape
    piece = width // 4
    packed = piece * 5 // 4
    left = pl.BlockSpec((piece, rows), lambda i, t: (i, 0))
    on_one = pl.BlockSpec((piece, rows), lambda i, t: (i * t[META + 1], 0))
    return pl.pallas_call(
        weight_kernel,
        grid_spec=pltpu.PrefetchScalarGridSpec(
            num_scalar_prefetch=1,
            grid=(4,),
            in_specs=[left, left, on_one, on_one] + [pl.BlockSpec(memory_space=pl.ANY)] * 4,
            out_specs=(
                pl.BlockSpec((None, 4, packed, 128), lambda i, t: (i, 0, 0, 0)),
                pl.BlockSpec((4, None, packed, 128), lambda i, t: (0, i, 0, 0)),
            ),
            scratch_shapes=[pltpu.VMEM((2 * rows, 2 * HW), bf16), pltpu.SemaphoreType.DMA((2,))],
        ),
        out_shape=(jax.ShapeDtypeStruct((4, 4, packed, 128), bf16),) * 2,
        compiler_params=params(),
        cost_estimate=cost(8 * width * rows * HW, 8 * width * rows + 4 * width * HW),
        name="weight_parts",
    )(table, normed, mate_normed, incoming, mate_incoming, *rights)


def unpacked(part):
    rest = part[320:]
    return jnp.concatenate(
        [part[:320], jnp.concatenate([rest[:, i * 32 : (i + 1) * 32] for i in range(4)], axis=0)], axis=1
    )


def to_mate(value):
    return lax.ppermute(value, "core", [(0, 1), (1, 0)])


def gathered(value, axis):
    count = AXES[axis]
    here = lax.axis_index(axis)
    out = jnp.zeros((count,) + value.shape, value.dtype)
    out = lax.dynamic_update_index_in_dim(out, value, here, 0)
    for k in range(1, count):
        part = lax.ppermute(value, axis, [(i, (i + k) % count) for i in range(count)])
        out = lax.dynamic_update_index_in_dim(out, part, lax.rem(here - k + count, count), 0)
    return out


def sent_to_owners(value, axis):
    count = AXES[axis]
    here = lax.axis_index(axis)
    parts = [lax.dynamic_index_in_dim(value, here, 0, keepdims=False)]
    for k in range(1, count):
        part = lax.dynamic_index_in_dim(value, lax.rem(here + k, count), 0, keepdims=False)
        parts.append(lax.ppermute(part, axis, [(i, (i + k) % count) for i in range(count)]))
    return parts


def added(parts):
    return sum(part.astype(f32) for part in parts)


def exchanged(value, axes):
    return lax.all_to_all(value, axes, split_axis=0, concat_axis=0, tiled=True)


def on_device(
    grad_rows,
    layer_input,
    saved_qkv,
    image_patches,
    image_owner,
    norm_gain,
    norm_bias,
    w_qkv,
    w_out,
):
    width = layer_input.shape[1]
    own_tiles = layer_input.shape[0] // TILE
    section = ("x", "core")
    sections = AXES["x"] * AXES["core"]
    core = lax.axis_index("core")
    place = jnp.stack([lax.axis_index(section), core]).astype(jnp.int32)

    columns = jnp.concatenate([w_out, lax.dynamic_slice_in_dim(w_qkv, 896 * core, 1024, axis=1)], axis=1)
    columns = gathered(columns, "y").reshape(4 * w_out.shape[0], HW + 1024)

    def gathered_z(value):
        return lax.all_gather(value, "z", axis=0, tiled=True)

    def in_order(whole):
        return jnp.swapaxes(whole.reshape(8, 4, -1, whole.shape[1]), 0, 1).reshape(whole.shape)

    table, outgoing = route(image_patches, image_owner, place, grad_rows, own_tiles, sections)
    arrived = exchanged(outgoing, section)
    out_w = gathered_z(columns[:, :HW])
    normed_t = norm_transposed(layer_input, norm_gain, norm_bias)
    attended, attended_t, weights = forward(table, saved_qkv)
    out_w, arrived, attended_t, normed_t, columns = lax.optimization_barrier(
        (out_w, arrived, attended_t, normed_t, columns)
    )
    mate_normed_t = to_mate(normed_t)
    out_w = in_order(out_w)
    qkv_w = gathered_z(columns[:, HW:])

    incoming, d_attn, incoming_t = place_incoming(table, arrived, out_w, own_tiles * TILE)
    mate_incoming_t = lax.ppermute(incoming_t, "core", [(0, 1)])
    value_query, attended_key = backward(table, saved_qkv, d_attn, attended, attended_t, weights)
    first, second = weight_parts(
        table,
        normed_t,
        mate_normed_t,
        incoming_t,
        mate_incoming_t,
        (
            value_query,
            attended_key,
            lax.ppermute(value_query, "core", [(1, 0)]),
            lax.ppermute(attended_key, "core", [(0, 1)]),
        ),
    )
    first, second, qkv_w = lax.optimization_barrier((first, second, qkv_w))
    qkv_w = in_order(qkv_w)
    layer_grad = norm_back(
        table, layer_input, incoming, norm_gain, value_query, attended_key, qkv_w, to_mate(qkv_w)
    )
    first = exchanged(first, "y")
    second = sent_to_owners(second, "x")
    first, second, layer_grad = lax.optimization_barrier((first, second, layer_grad))
    second = added(second).astype(bf16)
    first, second = lax.optimization_barrier((first, second))
    second = exchanged(second, "y")
    first = added(sent_to_owners(jnp.sum(first.astype(f32), axis=0).astype(bf16), "x"))
    second = jnp.sum(second.astype(f32), axis=0)
    columns = jnp.concatenate([unpacked(first), unpacked(second)], axis=1).astype(bf16)
    by_z = exchanged(columns.reshape(8, 40, 320), "z")
    share = jnp.sum(by_z.astype(f32), axis=0) / (AXES["y"] * AXES["z"] * sections)
    shares = gathered(gathered(share, "x"), "core")

    def assemble(core, first_column):
        mine = [shares[core, x][:, first_column : first_column + 160] for x in range(4)]
        return [part[:, :128] for part in mine] + [part[:, 128:] for part in mine]

    qkv_weight_grad = jnp.concatenate(assemble(0, 160) + assemble(1, 160) + assemble(0, 0), axis=1)
    out_weight_grad = jnp.concatenate(assemble(1, 0), axis=1)
    return layer_grad, qkv_weight_grad, out_weight_grad


def solution(mesh):
    fine = Mesh(mesh.devices.reshape(tuple(AXES.values())), tuple(AXES))
    rows = P(("y", "z", "x", "core"), None)
    dp = P(("y", "z"), None)
    return jax.shard_map(
        on_device,
        mesh=fine,
        in_specs=(rows, rows, rows, dp, dp, P(), P(), dp, dp),
        out_specs=(rows, dp, dp),
        check_vma=False,
    )
```

```python
import functools
import math

import jax
import jax.numpy as jnp
from jax import lax
from jax.experimental import pallas as pl
from jax.experimental.pallas import tpu as pltpu
from jax.sharding import Mesh, PartitionSpec as P

HEADS = 8
HEAD_DIM = 80
TILE = 128
WINDOW = 2 * TILE
HW = HEADS * HEAD_DIM
SCALE = 1.0 / math.sqrt(HEAD_DIM)
BLOCKS = 4
AXES = {"y": 4, "z": 8, "x": 4, "core": 2}
VMEM_LIMIT = 60 * 1024 * 1024

norm_eps = 1e-06
f32 = jnp.float32
bf16 = jnp.bfloat16

SOURCE, START, JOINED, META = 0, 8, 16, 24


def lane_window(head):
    first, last = head * HEAD_DIM, (head + 1) * HEAD_DIM
    return first // 128 * 128, -(-last // 128) * 128


def params():
    return pltpu.CompilerParams(vmem_limit_bytes=VMEM_LIMIT)


def cost(flops, moved):
    return pl.CostEstimate(flops=flops, bytes_accessed=moved, transcendentals=0)


def route_kernel(
    patches, owners, place, rows, table, outgoing, used, segment, own_owner, sems, *, own_tiles, src_tiles
):
    me = place[0]
    for j in range(8):
        used[j] = 0
        segment[j] = -1
        table[SOURCE + j] = -1
    for j in range(src_tiles):
        own_owner[j] = 0

    def image(i, begin):
        count = patches[0, i] // TILE
        owner = owners[0, i]
        slot = used[owner]
        used[owner] = slot + count
        for t in range(2):

            @pl.when(t < count)
            def _():
                position = begin + t
                source = position // src_tiles

                @pl.when(owner == me)
                def _():
                    table[SOURCE + slot + t] = source
                    segment[slot + t] = i

                @pl.when(source == me)
                def _():
                    own_owner[position % src_tiles] = owner

        return begin + count

    lax.fori_loop(0, patches.shape[1], image, jnp.int32(0))
    copies = []
    for j in range(src_tiles):
        first_row = pl.multiple_of(own_owner[j] * TILE, TILE)
        copy = pltpu.make_async_copy(
            rows.at[pl.ds(j * TILE, TILE)], outgoing.at[pl.ds(first_row, TILE)], sems.at[j]
        )
        copy.start()
        copies.append(copy)

    last = own_tiles - 1
    for b in range(8):
        table[START + b] = 0
        table[JOINED + b] = 0
        table[META + b] = 0
    table[META + 1] = place[1]
    table[META + 3] = place[2]

    def step(at):
        here = segment[at]
        after = segment[jnp.minimum(at + 1, last)]
        beyond = segment[jnp.minimum(at + 2, last)]
        joined = here == after
        splits = (at + 2 <= last) & (after == beyond) & jnp.logical_not(joined)
        return at + jnp.where(splits, 1, 2), joined

    def find(_, carry):
        at, lone = carry
        moved, _ = step(jnp.minimum(at, last))
        return jnp.where(at <= last, moved, at), lone | (at == last).astype(jnp.int32)

    _, lone = lax.fori_loop(0, BLOCKS, find, (jnp.int32(0), jnp.int32(0)))

    @pl.when(lone == 1)
    def _():
        table[START] = last - 1
        table[JOINED] = (segment[last - 1] == segment[last]).astype(jnp.int32)

    def block(_, carry):
        at, count = carry
        moved, joined = step(jnp.minimum(at, last))
        active = at < last

        @pl.when(active)
        def _():
            table[START + count] = at
            table[JOINED + count] = joined.astype(jnp.int32)

        return jnp.where(active, moved, at), count + active.astype(jnp.int32)

    _, count = lax.fori_loop(0, BLOCKS, block, (jnp.int32(0), lone))
    table[META] = count
    for copy in copies:
        copy.wait()


def route(patches, owners, place, rows, own_tiles, sections):
    src_tiles = rows.shape[0] // TILE
    smem = pl.BlockSpec(memory_space=pltpu.SMEM)
    hbm = pl.BlockSpec(memory_space=pl.ANY)
    return pl.pallas_call(
        functools.partial(route_kernel, own_tiles=own_tiles, src_tiles=src_tiles),
        out_shape=(
            jax.ShapeDtypeStruct((32,), jnp.int32),
            jax.ShapeDtypeStruct((sections * TILE, rows.shape[1]), bf16),
        ),
        in_specs=[smem, smem, smem, pl.BlockSpec(memory_space=pltpu.VMEM)],
        out_specs=(smem, hbm),
        scratch_shapes=[
            pltpu.SMEM((8,), jnp.int32),
            pltpu.SMEM((8,), jnp.int32),
            pltpu.SMEM((src_tiles,), jnp.int32),
            pltpu.SemaphoreType.DMA((src_tiles,)),
        ],
        compiler_params=params(),
        cost_estimate=cost(0, 4 * rows.size),
        name="route",
    )(patches, owners, place, rows)


def norm_kernel(x, gain, bias, out):
    wide = x[...].astype(f32)
    average = jnp.mean(wide, axis=1, keepdims=True)
    centered = wide - average
    inv_scale = lax.rsqrt(jnp.mean(centered * centered, axis=1, keepdims=True) + norm_eps)
    normed = centered * inv_scale * gain[...] + bias[...]
    out[...] = jnp.transpose(normed.astype(bf16))


def norm_transposed(x, gain, bias):
    rows, width = x.shape
    return pl.pallas_call(
        norm_kernel,
        grid=(rows // TILE,),
        out_shape=jax.ShapeDtypeStruct((width, rows), bf16),
        in_specs=[
            pl.BlockSpec((TILE, width), lambda t: (t, 0)),
            pl.BlockSpec((1, width), lambda t: (0, 0)),
            pl.BlockSpec((1, width), lambda t: (0, 0)),
        ],
        out_specs=pl.BlockSpec((width, TILE), lambda t: (0, t)),
        compiler_params=params(),
        cost_estimate=cost(10**6, 10**5),
        name="norm",
    )(x, gain.reshape(1, width), bias.reshape(1, width))


def padded_rows(values, head):
    low, high = lane_window(head)
    first = head * HEAD_DIM
    parts = []
    if first > low:
        parts.append(jnp.zeros((first - low, values.shape[1]), values.dtype))
    parts.append(values[first : first + HEAD_DIM])
    if high > first + HEAD_DIM:
        parts.append(jnp.zeros((high - first - HEAD_DIM, values.shape[1]), values.dtype))
    return jnp.concatenate(parts, axis=0) if len(parts) > 1 else parts[0]


def lane_mask(head):
    low, high = lane_window(head)
    lanes = lax.broadcasted_iota(jnp.int32, (1, high - low), 1) + low
    return ((lanes >= head * HEAD_DIM) & (lanes < (head + 1) * HEAD_DIM)).astype(f32).astype(bf16)


def matmul(a, b):
    return lax.dot_general(a, b, (((1,), (0,)), ((), ())), preferred_element_type=f32)


def block_at(rank):
    return lambda b, t: (jnp.minimum(b, jnp.maximum(t[META] - 1, 0)),) + (0,) * (rank - 1)


def softmax_over_rows(scores):
    scores = scores * (SCALE * math.log2(math.e))
    shifted = jnp.exp2(scores - jnp.max(scores, axis=0, keepdims=True))
    return (shifted * (1.0 / jnp.sum(shifted, axis=0, keepdims=True))).astype(bf16)


def forward_kernel(table, qkv, attended, attended_t, weights):
    b = pl.program_id(0)
    rows = pl.ds(pl.multiple_of(table[START + b] * TILE, TILE), WINDOW)
    joined = table[JOINED + b] == 1

    def attend(whole_window):
        queries_t = jnp.transpose(qkv[rows, 0:HW])
        values_t = jnp.transpose(qkv[rows, 2 * HW : 3 * HW])

        def scores_of(h):
            low, high = lane_window(h)
            return matmul(qkv[rows, HW + low : HW + high], padded_rows(queries_t, h))

        heads = []
        for h in range(HEADS):
            scores = scores_of(h)
            if whole_window:
                kept = softmax_over_rows(scores)
            else:
                nothing = jnp.zeros((TILE, TILE), bf16)
                top = softmax_over_rows(scores[:TILE, :TILE])
                bottom = softmax_over_rows(scores[TILE:, TILE:])
                kept = jnp.concatenate(
                    [
                        jnp.concatenate([top, nothing], axis=1),
                        jnp.concatenate([nothing, bottom], axis=1),
                    ],
                    axis=0,
                )
            weights[0, h] = kept
            heads.append(matmul(values_t[h * HEAD_DIM : (h + 1) * HEAD_DIM], kept).astype(bf16))
        whole = jnp.concatenate(heads, axis=0)
        attended_t[0] = whole
        attended[rows, :] = jnp.transpose(whole)

    pl.when((b < table[META]) & joined)(lambda: attend(True))
    pl.when((b < table[META]) & jnp.logical_not(joined))(lambda: attend(False))


def forward(table, qkv):
    rows, width = qkv.shape
    return pl.pallas_call(
        forward_kernel,
        grid_spec=pltpu.PrefetchScalarGridSpec(
            num_scalar_prefetch=1,
            grid=(BLOCKS,),
            in_specs=[pl.BlockSpec((rows, width), lambda b, t: (0, 0))],
            out_specs=(
                pl.BlockSpec((rows, HW), lambda b, t: (0, 0)),
                pl.BlockSpec((1, HW, WINDOW), block_at(3)),
                pl.BlockSpec((1, HEADS, WINDOW, WINDOW), block_at(4)),
            ),
        ),
        out_shape=(
            jax.ShapeDtypeStruct((rows, HW), bf16),
            jax.ShapeDtypeStruct((BLOCKS, HW, WINDOW), bf16),
            jax.ShapeDtypeStruct((BLOCKS, HEADS, WINDOW, WINDOW), bf16),
        ),
        compiler_params=params(),
        cost_estimate=cost(10**6, 10**5),
        name="attend",
    )(table, qkv)


def incoming_kernel(table, arrived, spread, incoming, d_attn, incoming_t, landing, w, sems, *, tiles):
    t = pl.program_id(0)
    places = AXES["y"]
    piece = spread.shape[0]

    def w_copy(y):
        return pltpu.make_async_copy(
            spread.at[:, pl.ds(y * HW, HW)], w.at[pl.ds(y * piece, piece)], sems.at[tiles + y]
        )

    def row_copy(j, source):
        first_row = pl.multiple_of(source * TILE, TILE)
        return pltpu.make_async_copy(
            arrived.at[pl.ds(first_row, TILE)], landing.at[pl.ds(j * TILE, TILE)], sems.at[j]
        )

    @pl.when(t == 0)
    def _():
        for y in range(places):
            w_copy(y).start()
        for j in range(tiles):
            source = table[SOURCE + j]

            @pl.when(source >= 0)
            def _():
                row_copy(j, source).start()

            @pl.when(source < 0)
            def _():
                landing[j * TILE : (j + 1) * TILE] = jnp.zeros((TILE, landing.shape[1]), bf16)

    for i in range(2):
        j = 2 * t + i
        pl.when(table[SOURCE + j] >= 0)(row_copy(j, 0).wait)
    rows = landing[pl.ds(pl.multiple_of(t * WINDOW, WINDOW), WINDOW)]
    incoming[...] = rows
    incoming_t[...] = jnp.transpose(rows)

    @pl.when(t == 0)
    def _():
        for y in range(places):
            w_copy(y).wait()

    d_attn[...] = matmul(rows, w[...]).astype(bf16)


def place_incoming(table, arrived, spread, rows):
    width = arrived.shape[1]
    return pl.pallas_call(
        functools.partial(incoming_kernel, tiles=rows // TILE),
        grid_spec=pltpu.PrefetchScalarGridSpec(
            num_scalar_prefetch=1,
            grid=(rows // WINDOW,),
            in_specs=[
                pl.BlockSpec(memory_space=pl.ANY),
                pl.BlockSpec(memory_space=pl.ANY),
            ],
            out_specs=(
                pl.BlockSpec((WINDOW, width), lambda i, t: (i, 0)),
                pl.BlockSpec((WINDOW, HW), lambda i, t: (i, 0)),
                pl.BlockSpec((width, WINDOW), lambda i, t: (0, i)),
            ),
            scratch_shapes=[
                pltpu.VMEM((rows, width), bf16),
                pltpu.VMEM((width, HW), bf16),
                pltpu.SemaphoreType.DMA((rows // TILE + AXES["y"],)),
            ],
        ),
        out_shape=(
            jax.ShapeDtypeStruct((rows, width), bf16),
            jax.ShapeDtypeStruct((rows, HW), bf16),
            jax.ShapeDtypeStruct((width, rows), bf16),
        ),
        compiler_params=params(),
        cost_estimate=cost(2 * rows * width * HW, 10 * rows * width),
        name="incoming",
    )(table, arrived, spread)


def add_lanes(tiles, low, part):
    for j in range(part.shape[1] // 128):
        piece = part[:, j * 128 : (j + 1) * 128]
        at = low // 128 + j
        tiles[at] = piece if tiles[at] is None else tiles[at] + piece


def backward_kernel(
    table, qkv, d_attn, attended, attended_t, weights, value_query, attended_key
):
    b = pl.program_id(0)

    @pl.when(b < table[META])
    def _():
        rows = pl.ds(pl.multiple_of(table[START + b] * TILE, TILE), WINDOW)
        grad_t = jnp.transpose(d_attn[rows, :])
        keys_t = jnp.transpose(qkv[rows, HW : 2 * HW])
        query_grads = []
        key_tiles = [None] * (HW // 128)
        value_tiles = [None] * (HW // 128)
        for h in range(HEADS):
            low, high = lane_window(h)
            mine = slice(h * HEAD_DIM, (h + 1) * HEAD_DIM)
            mask = lane_mask(h)
            prob_grad = matmul(qkv[rows, 2 * HW + low : 2 * HW + high], padded_rows(grad_t, h))
            row_delta = jnp.sum(
                grad_t[mine].astype(f32) * attended_t[0, mine].astype(f32), axis=0, keepdims=True
            )
            dscore = (weights[0, h].astype(f32) * ((prob_grad - row_delta) * SCALE)).astype(bf16)
            query_grads.append(matmul(keys_t[mine], dscore).astype(bf16))
            add_lanes(key_tiles, low, matmul(dscore, qkv[rows, low:high] * mask))
            add_lanes(value_tiles, low, matmul(weights[0, h], d_attn[rows, low:high] * mask))
        value_query[rows, HW:] = jnp.transpose(jnp.concatenate(query_grads, axis=0))
        for j in range(HW // 128):
            value_query[rows, j * 128 : (j + 1) * 128] = value_tiles[j].astype(bf16)
            attended_key[rows, HW + j * 128 : HW + (j + 1) * 128] = key_tiles[j].astype(bf16)
        attended_key[rows, :HW] = attended[rows, :]


def backward(table, qkv, d_attn, attended, attended_t, weights):
    rows, width = qkv.shape
    whole = pl.BlockSpec((rows, HW), lambda b, t: (0, 0))
    return pl.pallas_call(
        backward_kernel,
        grid_spec=pltpu.PrefetchScalarGridSpec(
            num_scalar_prefetch=1,
            grid=(BLOCKS,),
            in_specs=[
                pl.BlockSpec((rows, width), lambda b, t: (0, 0)),
                whole,
                whole,
                pl.BlockSpec((1, HW, WINDOW), block_at(3)),
                pl.BlockSpec((1, HEADS, WINDOW, WINDOW), block_at(4)),
            ],
            out_specs=(pl.BlockSpec((rows, 2 * HW), lambda b, t: (0, 0)),) * 2,
        ),
        out_shape=(jax.ShapeDtypeStruct((rows, 2 * HW), bf16),) * 2,
        compiler_params=params(),
        cost_estimate=cost(12 * 10**9, 20 * 10**6),
        name="attend_back",
    )(table, qkv, d_attn, attended, attended_t, weights)


def norm_back_kernel(table, x, incoming, gain, d_query, d_key, d_value, own_w, mate_w, out):
    def halves(low, high):
        grads = jnp.concatenate([d_query[...], d_key[...], d_value[...]], axis=1)
        contract = (((1,), (1,)), ((), ()))
        return lax.dot_general(
            grads[:, :1024], low[...], contract, preferred_element_type=f32
        ) + lax.dot_general(
            grads[:, 1024:], high[:, 128:1024], contract, preferred_element_type=f32
        )

    def finish(dnormed):
        wide = x[...].astype(f32)
        average = jnp.mean(wide, axis=1, keepdims=True)
        centered = wide - average
        inv_scale = lax.rsqrt(jnp.mean(centered * centered, axis=1, keepdims=True) + norm_eps)
        normalized = centered * inv_scale
        scaled_grad = dnormed * gain[...]
        branch = inv_scale * (
            scaled_grad
            - jnp.mean(scaled_grad, axis=1, keepdims=True)
            - normalized * jnp.mean(scaled_grad * normalized, axis=1, keepdims=True)
        )
        out[...] = (incoming[...].astype(f32) + branch).astype(bf16)

    first = table[META + 1] == 0

    @pl.when(first)
    def _():
        finish(halves(own_w, mate_w))

    @pl.when(jnp.logical_not(first))
    def _():
        finish(halves(mate_w, own_w))


def norm_back(table, x, incoming, gain, value_query, attended_key, own_w, mate_w):
    rows, width = x.shape
    wide = pl.BlockSpec((WINDOW, width), lambda i, t: (i, 0))
    weights = pl.BlockSpec((width, 1024), lambda i, t: (0, 0))
    return pl.pallas_call(
        norm_back_kernel,
        grid_spec=pltpu.PrefetchScalarGridSpec(
            num_scalar_prefetch=1,
            grid=(rows // WINDOW,),
            in_specs=[
                wide,
                wide,
                pl.BlockSpec((1, width), lambda i, t: (0, 0)),
                pl.BlockSpec((WINDOW, HW), lambda i, t: (i, 1)),
                pl.BlockSpec((WINDOW, HW), lambda i, t: (i, 1)),
                pl.BlockSpec((WINDOW, HW), lambda i, t: (i, 0)),
                weights,
                weights,
            ],
            out_specs=wide,
        ),
        out_shape=jax.ShapeDtypeStruct((rows, width), bf16),
        compiler_params=params(),
        cost_estimate=cost(2 * rows * width * 3 * HW, 20 * 10**6),
        name="norm_back",
    )(table, x, incoming, gain.reshape(1, width), value_query, attended_key, value_query, own_w, mate_w)


def packed_columns(total, store):
    rows = total.shape[0]
    group = rows // 4
    fifth = total[:, 512:640]
    quarter = lax.broadcasted_iota(jnp.int32, (group, 128), 1) // 32
    for x in range(4):
        packed = jnp.zeros((group, 128), f32)
        for g in range(4):
            piece = fifth[g * group : (g + 1) * group]
            shift = (g - x) * 32 % 128
            packed = jnp.where(quarter == g, pltpu.roll(piece, shift, 1) if shift else piece, packed)
        store(x, jnp.concatenate([total[:, x * 128 : (x + 1) * 128], packed], axis=0).astype(bf16))


def weight_kernel(
    table, normed, mate_normed, incoming, mate_incoming, zero, one, mate_zero, mate_one, by_y, by_x, right, sems
):
    first = table[META + 1] == 0
    depth = zero.shape[0]

    def copy(side, source):
        return pltpu.make_async_copy(source, right.at[pl.ds(side * depth, depth)], sems.at[side])

    @pl.when(pl.program_id(0) == 0)
    def _():
        for side, (on_zero, on_one) in enumerate(((zero, one), (mate_zero, mate_one))):
            pl.when(first)(copy(side, on_zero).start)
            pl.when(jnp.logical_not(first))(copy(side, on_one).start)
        for side in range(2):
            copy(side, zero).wait()

    normed_both = jnp.concatenate([normed[...], mate_normed[...]], axis=1)
    incoming_both = jnp.concatenate([incoming[...], mate_incoming[...]], axis=1)
    left = jnp.where(first, normed_both, incoming_both)
    to_y, to_x = matmul(left, right[:, :HW]), matmul(normed_both, right[:, HW:])
    piece = to_y.shape[0] // 2
    for i in range(2):

        def store_y(x, value):
            by_y[i, x] = value

        def store_x(x, value):
            by_x[lax.rem(x - table[META + 3] + 4, 4), i] = value

        packed_columns(to_y[i * piece : (i + 1) * piece], store_y)
        packed_columns(to_x[i * piece : (i + 1) * piece], store_x)


def weight_parts(table, normed, mate_normed, incoming, mate_incoming, rights):
    width, rows = normed.shape
    piece = width // 4
    packed = piece * 5 // 4
    left = pl.BlockSpec((2 * piece, rows), lambda i, t: (i, 0))
    on_one = pl.BlockSpec((2 * piece, rows), lambda i, t: (i * t[META + 1], 0))
    return pl.pallas_call(
        weight_kernel,
        grid_spec=pltpu.PrefetchScalarGridSpec(
            num_scalar_prefetch=1,
            grid=(2,),
            in_specs=[left, left, on_one, on_one] + [pl.BlockSpec(memory_space=pl.ANY)] * 4,
            out_specs=(
                pl.BlockSpec((2, 4, packed, 128), lambda i, t: (i, 0, 0, 0)),
                pl.BlockSpec((4, 2, packed, 128), lambda i, t: (0, i, 0, 0)),
            ),
            scratch_shapes=[pltpu.VMEM((2 * rows, 2 * HW), bf16), pltpu.SemaphoreType.DMA((2,))],
        ),
        out_shape=(jax.ShapeDtypeStruct((4, 4, packed, 128), bf16),) * 2,
        compiler_params=params(),
        cost_estimate=cost(8 * width * rows * HW, 8 * width * rows + 4 * width * HW),
        name="weight_parts",
    )(table, normed, mate_normed, incoming, mate_incoming, *rights)


def unpacked(part):
    rest = part[320:]
    return jnp.concatenate(
        [part[:320], jnp.concatenate([rest[:, i * 32 : (i + 1) * 32] for i in range(4)], axis=0)], axis=1
    )


def to_mate(value):
    return lax.ppermute(value, "core", [(0, 1), (1, 0)])


def gathered(value, axis):
    count = AXES[axis]
    here = lax.axis_index(axis)
    out = jnp.zeros((count,) + value.shape, value.dtype)
    out = lax.dynamic_update_index_in_dim(out, value, here, 0)
    for k in range(1, count):
        part = lax.ppermute(value, axis, [(i, (i + k) % count) for i in range(count)])
        out = lax.dynamic_update_index_in_dim(out, part, lax.rem(here - k + count, count), 0)
    return out


def sent_by_distance(value, axis):
    count = AXES[axis]
    return [value[0]] + [
        lax.ppermute(value[k], axis, [(i, (i + k) % count) for i in range(count)])
        for k in range(1, count)
    ]


def by_distance(value, axis):
    return jnp.roll(value, -lax.axis_index(axis), axis=0)


def added(parts):
    return sum(part.astype(f32) for part in parts)


def exchanged(value, axes):
    return lax.all_to_all(value, axes, split_axis=0, concat_axis=0, tiled=True)


def on_device(
    grad_rows,
    layer_input,
    saved_qkv,
    image_patches,
    image_owner,
    norm_gain,
    norm_bias,
    w_qkv,
    w_out,
):
    width = layer_input.shape[1]
    own_tiles = layer_input.shape[0] // TILE
    section = ("x", "core")
    sections = AXES["x"] * AXES["core"]
    core = lax.axis_index("core")
    place = jnp.stack([lax.axis_index(section), core, lax.axis_index("x")]).astype(jnp.int32)

    spread = gathered(w_out, "y")
    spread = jnp.concatenate(
        [spread[y] for y in range(4)] + [lax.dynamic_slice_in_dim(w_qkv, 896 * core, 1024, axis=1)], axis=1
    )
    table, outgoing = route(image_patches, image_owner, place, grad_rows, own_tiles, sections)
    arrived = exchanged(outgoing, section)
    spread = lax.all_gather(spread, "z", axis=0, tiled=True)
    normed_t = norm_transposed(layer_input, norm_gain, norm_bias)
    mate_normed_t = to_mate(normed_t)
    attended, attended_t, weights = forward(table, saved_qkv)
    spread, arrived, attended_t, normed_t = lax.optimization_barrier(
        (spread, arrived, attended_t, normed_t)
    )
    qkv_w = lax.all_gather(spread[:, 4 * HW :], "y", axis=0, tiled=True)

    incoming, d_attn, incoming_t = place_incoming(table, arrived, spread, own_tiles * TILE)
    mate_incoming_t = lax.ppermute(incoming_t, "core", [(0, 1)])
    d_attn, mate_normed_t = lax.optimization_barrier((d_attn, mate_normed_t))
    value_query, attended_key = backward(table, saved_qkv, d_attn, attended, attended_t, weights)
    first, second = weight_parts(
        table,
        normed_t,
        mate_normed_t,
        incoming_t,
        mate_incoming_t,
        (
            value_query,
            attended_key,
            lax.ppermute(value_query, "core", [(1, 0)]),
            lax.ppermute(attended_key, "core", [(0, 1)]),
        ),
    )
    first, second, qkv_w = lax.optimization_barrier((first, second, qkv_w))
    layer_grad = norm_back(
        table, layer_input, incoming, norm_gain, value_query, attended_key, qkv_w, to_mate(qkv_w)
    )
    first = exchanged(first, "y")
    second = sent_by_distance(second, "x")
    first, second, layer_grad = lax.optimization_barrier((first, second, layer_grad))
    second = added(second).astype(bf16)
    first, second = lax.optimization_barrier((first, second))
    second = exchanged(second, "y")
    first = by_distance(jnp.sum(first.astype(f32), axis=0).astype(bf16), "x")
    first = sent_by_distance(first, "x")
    second = jnp.sum(second.astype(f32), axis=0)
    first, second = lax.optimization_barrier((first, second))
    first = added(first)
    columns = jnp.concatenate([unpacked(first), unpacked(second)], axis=1).astype(bf16)
    by_z = exchanged(columns.reshape(8, 40, 320), "z")
    share = jnp.sum(by_z.astype(f32), axis=0) / (AXES["y"] * AXES["z"] * sections)
    shares = gathered(gathered(share, "x"), "core")

    def assemble(core, first_column):
        mine = [shares[core, x][:, first_column : first_column + 160] for x in range(4)]
        return [part[:, :128] for part in mine] + [part[:, 128:] for part in mine]

    qkv_weight_grad = jnp.concatenate(assemble(0, 160) + assemble(1, 160) + assemble(0, 0), axis=1)
    out_weight_grad = jnp.concatenate(assemble(1, 0), axis=1)
    return layer_grad, qkv_weight_grad, out_weight_grad


def solution(mesh):
    fine = Mesh(mesh.devices.reshape(tuple(AXES.values())), tuple(AXES))
    rows = P(("y", "z", "x", "core"), None)
    dp = P(("y", "z"), None)
    return jax.shard_map(
        on_device,
        mesh=fine,
        in_specs=(rows, rows, rows, dp, dp, P(), P(), dp, dp),
        out_specs=(rows, dp, dp),
        check_vma=False,
    )
```

```python
import functools
import math

import jax
import jax.numpy as jnp
from jax import lax
from jax.experimental import pallas as pl
from jax.experimental.pallas import tpu as pltpu
from jax.sharding import Mesh, PartitionSpec as P

HEADS = 8
HEAD_DIM = 80
TILE = 128
WINDOW = 2 * TILE
HW = HEADS * HEAD_DIM
SCALE = 1.0 / math.sqrt(HEAD_DIM)
BLOCKS = 4
QKV_PART = 1024
AXES = {"y": 4, "z": 8, "x": 4, "core": 2}
VMEM_LIMIT = 60 * 1024 * 1024

norm_eps = 1e-06
f32 = jnp.float32
bf16 = jnp.bfloat16

SOURCE, START, JOINED, META = 0, 8, 16, 24


def lane_window(head):
    first, last = head * HEAD_DIM, (head + 1) * HEAD_DIM
    return first // 128 * 128, -(-last // 128) * 128


def params():
    return pltpu.CompilerParams(vmem_limit_bytes=VMEM_LIMIT)


def cost(flops, moved):
    return pl.CostEstimate(flops=flops, bytes_accessed=moved, transcendentals=0)


def route_kernel(
    patches, owners, place, rows, table, outgoing, used, segment, own_owner, sems, *, own_tiles, src_tiles
):
    me = place[0]
    for j in range(8):
        used[j] = 0
        segment[j] = -1
        table[SOURCE + j] = -1
    for j in range(src_tiles):
        own_owner[j] = 0

    def image(i, begin):
        count = patches[0, i] // TILE
        owner = owners[0, i]
        slot = used[owner]
        used[owner] = slot + count
        for t in range(2):

            @pl.when(t < count)
            def _():
                position = begin + t
                source = position // src_tiles

                @pl.when(owner == me)
                def _():
                    table[SOURCE + slot + t] = source
                    segment[slot + t] = i

                @pl.when(source == me)
                def _():
                    own_owner[position % src_tiles] = owner

        return begin + count

    lax.fori_loop(0, patches.shape[1], image, jnp.int32(0))
    copies = []
    for j in range(src_tiles):
        first_row = pl.multiple_of(own_owner[j] * TILE, TILE)
        copy = pltpu.make_async_copy(
            rows.at[pl.ds(j * TILE, TILE)], outgoing.at[pl.ds(first_row, TILE)], sems.at[j]
        )
        copy.start()
        copies.append(copy)

    last = own_tiles - 1
    for b in range(8):
        table[START + b] = 0
        table[JOINED + b] = 0
        table[META + b] = 0
    table[META + 1] = place[1]
    table[META + 3] = place[2]

    def step(at):
        here = segment[at]
        after = segment[jnp.minimum(at + 1, last)]
        beyond = segment[jnp.minimum(at + 2, last)]
        joined = here == after
        splits = (at + 2 <= last) & (after == beyond) & jnp.logical_not(joined)
        return at + jnp.where(splits, 1, 2), joined

    def find(_, carry):
        at, lone = carry
        moved, _ = step(jnp.minimum(at, last))
        return jnp.where(at <= last, moved, at), lone | (at == last).astype(jnp.int32)

    _, lone = lax.fori_loop(0, BLOCKS, find, (jnp.int32(0), jnp.int32(0)))

    @pl.when(lone == 1)
    def _():
        table[START] = last - 1
        table[JOINED] = (segment[last - 1] == segment[last]).astype(jnp.int32)

    def block(_, carry):
        at, count = carry
        moved, joined = step(jnp.minimum(at, last))
        active = at < last

        @pl.when(active)
        def _():
            table[START + count] = at
            table[JOINED + count] = joined.astype(jnp.int32)

        return jnp.where(active, moved, at), count + active.astype(jnp.int32)

    _, count = lax.fori_loop(0, BLOCKS, block, (jnp.int32(0), lone))
    table[META] = count
    for copy in copies:
        copy.wait()


def route(patches, owners, place, rows, own_tiles, sections):
    src_tiles = rows.shape[0] // TILE
    smem = pl.BlockSpec(memory_space=pltpu.SMEM)
    hbm = pl.BlockSpec(memory_space=pl.ANY)
    return pl.pallas_call(
        functools.partial(route_kernel, own_tiles=own_tiles, src_tiles=src_tiles),
        out_shape=(
            jax.ShapeDtypeStruct((32,), jnp.int32),
            jax.ShapeDtypeStruct((sections * TILE, rows.shape[1]), bf16),
        ),
        in_specs=[smem, smem, smem, pl.BlockSpec(memory_space=pltpu.VMEM)],
        out_specs=(smem, hbm),
        scratch_shapes=[
            pltpu.SMEM((8,), jnp.int32),
            pltpu.SMEM((8,), jnp.int32),
            pltpu.SMEM((src_tiles,), jnp.int32),
            pltpu.SemaphoreType.DMA((src_tiles,)),
        ],
        compiler_params=params(),
        cost_estimate=cost(0, 4 * rows.size),
        name="route",
    )(patches, owners, place, rows)


def norm_kernel(x, gain, bias, out):
    wide = x[...].astype(f32)
    average = jnp.mean(wide, axis=1, keepdims=True)
    centered = wide - average
    inv_scale = lax.rsqrt(jnp.mean(centered * centered, axis=1, keepdims=True) + norm_eps)
    normed = centered * inv_scale * gain[...] + bias[...]
    out[...] = jnp.transpose(normed.astype(bf16))


def norm_transposed(x, gain, bias):
    rows, width = x.shape
    return pl.pallas_call(
        norm_kernel,
        grid=(rows // TILE,),
        out_shape=jax.ShapeDtypeStruct((width, rows), bf16),
        in_specs=[
            pl.BlockSpec((TILE, width), lambda t: (t, 0)),
            pl.BlockSpec((1, width), lambda t: (0, 0)),
            pl.BlockSpec((1, width), lambda t: (0, 0)),
        ],
        out_specs=pl.BlockSpec((width, TILE), lambda t: (0, t)),
        compiler_params=params(),
        cost_estimate=cost(10**6, 10**5),
        name="norm",
    )(x, gain.reshape(1, width), bias.reshape(1, width))


def padded_rows(values, head):
    low, high = lane_window(head)
    first = head * HEAD_DIM
    parts = []
    if first > low:
        parts.append(jnp.zeros((first - low, values.shape[1]), values.dtype))
    parts.append(values[first : first + HEAD_DIM])
    if high > first + HEAD_DIM:
        parts.append(jnp.zeros((high - first - HEAD_DIM, values.shape[1]), values.dtype))
    return jnp.concatenate(parts, axis=0) if len(parts) > 1 else parts[0]


def lane_mask(head):
    low, high = lane_window(head)
    lanes = lax.broadcasted_iota(jnp.int32, (1, high - low), 1) + low
    return ((lanes >= head * HEAD_DIM) & (lanes < (head + 1) * HEAD_DIM)).astype(f32).astype(bf16)


def matmul(a, b):
    return lax.dot_general(a, b, (((1,), (0,)), ((), ())), preferred_element_type=f32)


def block_at(rank):
    return lambda b, t: (jnp.minimum(b, jnp.maximum(t[META] - 1, 0)),) + (0,) * (rank - 1)


def softmax_over_rows(scores):
    scores = scores * (SCALE * math.log2(math.e))
    shifted = jnp.exp2(scores - jnp.max(scores, axis=0, keepdims=True))
    return (shifted * (1.0 / jnp.sum(shifted, axis=0, keepdims=True))).astype(bf16)


def forward_kernel(table, qkv, attended, attended_t, weights):
    b = pl.program_id(0)
    rows = pl.ds(pl.multiple_of(table[START + b] * TILE, TILE), WINDOW)
    joined = table[JOINED + b] == 1

    def attend(whole_window):
        queries_t = jnp.transpose(qkv[rows, 0:HW])
        values_t = jnp.transpose(qkv[rows, 2 * HW : 3 * HW])

        def scores_of(h):
            low, high = lane_window(h)
            return matmul(qkv[rows, HW + low : HW + high], padded_rows(queries_t, h))

        heads = []
        for h in range(HEADS):
            scores = scores_of(h)
            if whole_window:
                kept = softmax_over_rows(scores)
            else:
                nothing = jnp.zeros((TILE, TILE), bf16)
                top = softmax_over_rows(scores[:TILE, :TILE])
                bottom = softmax_over_rows(scores[TILE:, TILE:])
                kept = jnp.concatenate(
                    [
                        jnp.concatenate([top, nothing], axis=1),
                        jnp.concatenate([nothing, bottom], axis=1),
                    ],
                    axis=0,
                )
            weights[0, h] = kept
            heads.append(matmul(values_t[h * HEAD_DIM : (h + 1) * HEAD_DIM], kept).astype(bf16))
        whole = jnp.concatenate(heads, axis=0)
        attended_t[0] = whole
        attended[rows, :] = jnp.transpose(whole)

    pl.when((b < table[META]) & joined)(lambda: attend(True))
    pl.when((b < table[META]) & jnp.logical_not(joined))(lambda: attend(False))


def forward(table, qkv):
    rows, width = qkv.shape
    return pl.pallas_call(
        forward_kernel,
        grid_spec=pltpu.PrefetchScalarGridSpec(
            num_scalar_prefetch=1,
            grid=(BLOCKS,),
            in_specs=[pl.BlockSpec((rows, width), lambda b, t: (0, 0))],
            out_specs=(
                pl.BlockSpec((rows, HW), lambda b, t: (0, 0)),
                pl.BlockSpec((1, HW, WINDOW), block_at(3)),
                pl.BlockSpec((1, HEADS, WINDOW, WINDOW), block_at(4)),
            ),
        ),
        out_shape=(
            jax.ShapeDtypeStruct((rows, HW), bf16),
            jax.ShapeDtypeStruct((BLOCKS, HW, WINDOW), bf16),
            jax.ShapeDtypeStruct((BLOCKS, HEADS, WINDOW, WINDOW), bf16),
        ),
        compiler_params=params(),
        cost_estimate=cost(10**6, 10**5),
        name="attend",
    )(table, qkv)


def incoming_kernel(
    table, arrived, spread, qkv_in, incoming, d_attn, incoming_t, qkv_out, landing, w, sems, *, tiles
):
    t = pl.program_id(0)
    places = AXES["y"]
    piece = spread.shape[0]

    def w_copy(y):
        return pltpu.make_async_copy(
            spread.at[:, pl.ds(QKV_PART + y * HW, HW)], w.at[pl.ds(y * piece, piece)], sems.at[tiles + y]
        )

    def row_copy(j, source):
        first_row = pl.multiple_of(source * TILE, TILE)
        return pltpu.make_async_copy(
            arrived.at[pl.ds(first_row, TILE)], landing.at[pl.ds(j * TILE, TILE)], sems.at[j]
        )

    @pl.when(t == 0)
    def _():
        for y in range(places):
            w_copy(y).start()
        for j in range(tiles):
            source = table[SOURCE + j]

            @pl.when(source >= 0)
            def _():
                row_copy(j, source).start()

            @pl.when(source < 0)
            def _():
                landing[j * TILE : (j + 1) * TILE] = jnp.zeros((TILE, landing.shape[1]), bf16)

    for i in range(2):
        j = 2 * t + i
        pl.when(table[SOURCE + j] >= 0)(row_copy(j, 0).wait)
    rows = landing[pl.ds(pl.multiple_of(t * WINDOW, WINDOW), WINDOW)]
    incoming[...] = rows
    incoming_t[...] = jnp.transpose(rows)

    @pl.when(t == 0)
    def _():
        qkv_out[...] = qkv_in[...]
        for y in range(places):
            w_copy(y).wait()

    d_attn[...] = matmul(rows, w[...]).astype(bf16)


def place_incoming(table, arrived, spread, rows):
    width = arrived.shape[1]
    qkv_part = pl.BlockSpec((spread.shape[0], QKV_PART), lambda i, t: (0, 0))
    return pl.pallas_call(
        functools.partial(incoming_kernel, tiles=rows // TILE),
        grid_spec=pltpu.PrefetchScalarGridSpec(
            num_scalar_prefetch=1,
            grid=(rows // WINDOW,),
            in_specs=[
                pl.BlockSpec(memory_space=pl.ANY),
                pl.BlockSpec(memory_space=pl.ANY),
                qkv_part,
            ],
            out_specs=(
                pl.BlockSpec((WINDOW, width), lambda i, t: (i, 0)),
                pl.BlockSpec((WINDOW, HW), lambda i, t: (i, 0)),
                pl.BlockSpec((width, WINDOW), lambda i, t: (0, i)),
                qkv_part,
            ),
            scratch_shapes=[
                pltpu.VMEM((rows, width), bf16),
                pltpu.VMEM((width, HW), bf16),
                pltpu.SemaphoreType.DMA((rows // TILE + AXES["y"],)),
            ],
        ),
        out_shape=(
            jax.ShapeDtypeStruct((rows, width), bf16),
            jax.ShapeDtypeStruct((rows, HW), bf16),
            jax.ShapeDtypeStruct((width, rows), bf16),
            jax.ShapeDtypeStruct((spread.shape[0], QKV_PART), bf16),
        ),
        compiler_params=params(),
        cost_estimate=cost(2 * rows * width * HW, 10 * rows * width),
        name="incoming",
    )(table, arrived, spread, spread)


def add_lanes(tiles, low, part):
    for j in range(part.shape[1] // 128):
        piece = part[:, j * 128 : (j + 1) * 128]
        at = low // 128 + j
        tiles[at] = piece if tiles[at] is None else tiles[at] + piece


def backward_kernel(table, qkv, d_attn, attended, attended_t, weights, own, send):
    b = pl.program_id(0)
    rows = pl.ds(pl.multiple_of(table[START + b] * TILE, TILE), WINDOW)
    joined = table[JOINED + b] == 1
    first = table[META + 1] == 0

    def grads(whole_window):
        grad_t = jnp.transpose(d_attn[rows, :])
        keys_t = jnp.transpose(qkv[rows, HW : 2 * HW])
        query_grads = []
        key_tiles = [None] * (HW // 128)
        value_tiles = [None] * (HW // 128)
        for h in range(HEADS):
            low, high = lane_window(h)
            mine = slice(h * HEAD_DIM, (h + 1) * HEAD_DIM)
            mask = lane_mask(h)
            prob_grad = matmul(qkv[rows, 2 * HW + low : 2 * HW + high], padded_rows(grad_t, h))
            row_delta = jnp.sum(
                grad_t[mine].astype(f32) * attended_t[0, mine].astype(f32), axis=0, keepdims=True
            )

            def score_grad(keys, queries):
                change = (prob_grad[keys, queries] - row_delta[:, queries]) * SCALE
                return (weights[0, h, keys, queries].astype(f32) * change).astype(bf16)

            if whole_window:
                dscore = score_grad(slice(0, WINDOW), slice(0, WINDOW))
            else:
                nothing = jnp.zeros((TILE, TILE), bf16)
                top = score_grad(slice(0, TILE), slice(0, TILE))
                bottom = score_grad(slice(TILE, WINDOW), slice(TILE, WINDOW))
                dscore = jnp.concatenate(
                    [
                        jnp.concatenate([top, nothing], axis=1),
                        jnp.concatenate([nothing, bottom], axis=1),
                    ],
                    axis=0,
                )
            query_grads.append(matmul(keys_t[mine], dscore).astype(bf16))
            add_lanes(key_tiles, low, matmul(dscore, qkv[rows, low:high] * mask))
            add_lanes(value_tiles, low, matmul(weights[0, h], d_attn[rows, low:high] * mask))

        def store(lanes, on_zero, on_one):
            own[rows, lanes] = jnp.where(first, on_zero, on_one)
            send[rows, lanes] = jnp.where(first, on_one, on_zero)

        d_query = jnp.transpose(jnp.concatenate(query_grads, axis=0))
        for j in range(HW // 128):
            lanes = slice(j * 128, (j + 1) * 128)
            store(lanes, value_tiles[j].astype(bf16), attended[rows, lanes])
            store(
                slice(HW + j * 128, HW + (j + 1) * 128), d_query[:, lanes], key_tiles[j].astype(bf16)
            )

    pl.when((b < table[META]) & joined)(lambda: grads(True))
    pl.when((b < table[META]) & jnp.logical_not(joined))(lambda: grads(False))


def backward(table, qkv, d_attn, attended, attended_t, weights):
    rows, width = qkv.shape
    whole = pl.BlockSpec((rows, HW), lambda b, t: (0, 0))
    return pl.pallas_call(
        backward_kernel,
        grid_spec=pltpu.PrefetchScalarGridSpec(
            num_scalar_prefetch=1,
            grid=(BLOCKS,),
            in_specs=[
                pl.BlockSpec((rows, width), lambda b, t: (0, 0)),
                whole,
                whole,
                pl.BlockSpec((1, HW, WINDOW), block_at(3)),
                pl.BlockSpec((1, HEADS, WINDOW, WINDOW), block_at(4)),
            ],
            out_specs=(pl.BlockSpec((rows, 2 * HW), lambda b, t: (0, 0)),) * 2,
        ),
        out_shape=(jax.ShapeDtypeStruct((rows, 2 * HW), bf16),) * 2,
        compiler_params=params(),
        cost_estimate=cost(12 * 10**9, 20 * 10**6),
        name="attend_back",
    )(table, qkv, d_attn, attended, attended_t, weights)


def norm_back_kernel(table, x, incoming, gain, own, send, own_w, mate_w, out):
    def halves(value_query, attended_key, low, high):
        grads = jnp.concatenate(
            [value_query[:, HW:], attended_key[:, HW:], value_query[:, :HW]], axis=1
        )
        contract = (((1,), (1,)), ((), ()))
        return lax.dot_general(
            grads[:, :1024], low[...], contract, preferred_element_type=f32
        ) + lax.dot_general(
            grads[:, 1024:], high[:, 128:1024], contract, preferred_element_type=f32
        )

    def finish(dnormed):
        wide = x[...].astype(f32)
        average = jnp.mean(wide, axis=1, keepdims=True)
        centered = wide - average
        inv_scale = lax.rsqrt(jnp.mean(centered * centered, axis=1, keepdims=True) + norm_eps)
        normalized = centered * inv_scale
        scaled_grad = dnormed * gain[...]
        branch = inv_scale * (
            scaled_grad
            - jnp.mean(scaled_grad, axis=1, keepdims=True)
            - normalized * jnp.mean(scaled_grad * normalized, axis=1, keepdims=True)
        )
        out[...] = (incoming[...].astype(f32) + branch).astype(bf16)

    first = table[META + 1] == 0

    @pl.when(first)
    def _():
        finish(halves(own, send, own_w, mate_w))

    @pl.when(jnp.logical_not(first))
    def _():
        finish(halves(send, own, mate_w, own_w))


def norm_back(table, x, incoming, gain, own, send, own_w, mate_w):
    rows, width = x.shape
    wide = pl.BlockSpec((WINDOW, width), lambda i, t: (i, 0))
    weights = pl.BlockSpec((width, 1024), lambda i, t: (0, 0))
    return pl.pallas_call(
        norm_back_kernel,
        grid_spec=pltpu.PrefetchScalarGridSpec(
            num_scalar_prefetch=1,
            grid=(rows // WINDOW,),
            in_specs=[
                wide,
                wide,
                pl.BlockSpec((1, width), lambda i, t: (0, 0)),
                pl.BlockSpec((WINDOW, 2 * HW), lambda i, t: (i, 0)),
                pl.BlockSpec((WINDOW, 2 * HW), lambda i, t: (i, 0)),
                weights,
                weights,
            ],
            out_specs=wide,
        ),
        out_shape=jax.ShapeDtypeStruct((rows, width), bf16),
        compiler_params=params(),
        cost_estimate=cost(2 * rows * width * 3 * HW, 20 * 10**6),
        name="norm_back",
    )(table, x, incoming, gain.reshape(1, width), own, send, own_w, mate_w)


def packed_columns(total, store):
    rows = total.shape[0]
    group = rows // 4
    fifth = total[:, 512:640]
    quarter = lax.broadcasted_iota(jnp.int32, (group, 128), 1) // 32
    for x in range(4):
        packed = jnp.zeros((group, 128), f32)
        for g in range(4):
            piece = fifth[g * group : (g + 1) * group]
            shift = (g - x) * 32 % 128
            packed = jnp.where(quarter == g, pltpu.roll(piece, shift, 1) if shift else piece, packed)
        store(x, jnp.concatenate([total[:, x * 128 : (x + 1) * 128], packed], axis=0).astype(bf16))


def weight_kernel(table, normed, mate_normed, incoming, mate_incoming, own, mate, by_y, by_x):
    first = table[META + 1] == 0
    left = jnp.where(first, normed[...], incoming[...])
    mate_left = jnp.where(first, mate_normed[...], mate_incoming[...])
    to_x = matmul(normed[...], own[:, HW:]) + matmul(mate_normed[...], mate[:, HW:])
    to_y = matmul(left, own[:, :HW]) + matmul(mate_left, mate[:, :HW])

    def store_x(x, value):
        by_x[lax.rem(x - table[META + 3] + 4, 4)] = value

    def store_y(x, value):
        by_y[x] = value

    packed_columns(to_x, store_x)
    packed_columns(to_y, store_y)


def weight_parts(table, normed, mate_normed, incoming, mate_incoming, own, mate):
    width, rows = normed.shape
    piece = width // 4
    packed = piece * 5 // 4
    left = pl.BlockSpec((piece, rows), lambda i, t: (i, 0))
    on_one = pl.BlockSpec((piece, rows), lambda i, t: (i * t[META + 1], 0))
    right = pl.BlockSpec((rows, 2 * HW), lambda i, t: (0, 0))
    return pl.pallas_call(
        weight_kernel,
        grid_spec=pltpu.PrefetchScalarGridSpec(
            num_scalar_prefetch=1,
            grid=(4,),
            in_specs=[left, left, on_one, on_one, right, right],
            out_specs=(
                pl.BlockSpec((None, 4, packed, 128), lambda i, t: (i, 0, 0, 0)),
                pl.BlockSpec((4, None, packed, 128), lambda i, t: (0, i, 0, 0)),
            ),
        ),
        out_shape=(jax.ShapeDtypeStruct((4, 4, packed, 128), bf16),) * 2,
        compiler_params=params(),
        cost_estimate=cost(8 * width * rows * HW, 8 * width * rows + 4 * width * HW),
        name="weight_parts",
    )(table, normed, mate_normed, incoming, mate_incoming, own, mate)


def unpacked(part):
    rest = part[320:]
    return jnp.concatenate(
        [part[:320], jnp.concatenate([rest[:, i * 32 : (i + 1) * 32] for i in range(4)], axis=0)], axis=1
    )


def to_mate(value):
    return lax.ppermute(value, "core", [(0, 1), (1, 0)])


def gathered(value, axis):
    count = AXES[axis]
    here = lax.axis_index(axis)
    out = jnp.zeros((count,) + value.shape, value.dtype)
    out = lax.dynamic_update_index_in_dim(out, value, here, 0)
    for k in range(1, count):
        part = lax.ppermute(value, axis, [(i, (i + k) % count) for i in range(count)])
        out = lax.dynamic_update_index_in_dim(out, part, lax.rem(here - k + count, count), 0)
    return out


def sent_by_distance(parts, axis):
    count = AXES[axis]
    return [parts[0]] + [
        lax.ppermute(parts[k], axis, [(i, (i + k) % count) for i in range(count)])
        for k in range(1, count)
    ]


def by_distance(value, axis):
    return jnp.roll(value, -lax.axis_index(axis), axis=0)


def added(parts):
    return sum(part.astype(f32) for part in parts)


def exchanged(value, axes):
    return lax.all_to_all(value, axes, split_axis=0, concat_axis=0, tiled=True)


def on_device(
    grad_rows,
    layer_input,
    saved_qkv,
    image_patches,
    image_owner,
    norm_gain,
    norm_bias,
    w_qkv,
    w_out,
):
    width = layer_input.shape[1]
    own_tiles = layer_input.shape[0] // TILE
    section = ("x", "core")
    sections = AXES["x"] * AXES["core"]
    core = lax.axis_index("core")
    place = jnp.stack([lax.axis_index(section), core, lax.axis_index("x")]).astype(jnp.int32)

    spread = gathered(w_out, "y")
    spread = jnp.concatenate(
        [lax.dynamic_slice_in_dim(w_qkv, 896 * core, QKV_PART, axis=1)] + [spread[y] for y in range(4)], axis=1
    )
    table, outgoing = route(image_patches, image_owner, place, grad_rows, own_tiles, sections)
    arrived = exchanged(outgoing, section)
    spread = lax.all_gather(spread, "z", axis=0, tiled=True)
    normed_t = norm_transposed(layer_input, norm_gain, norm_bias)
    mate_normed_t = to_mate(normed_t)
    attended, attended_t, weights = forward(table, saved_qkv)
    spread, arrived, attended_t, normed_t = lax.optimization_barrier(
        (spread, arrived, attended_t, normed_t)
    )
    incoming, d_attn, incoming_t, qkv_w = place_incoming(table, arrived, spread, own_tiles * TILE)
    qkv_w = lax.all_gather(qkv_w, "y", axis=0, tiled=True)
    mate_incoming_t = to_mate(incoming_t)
    d_attn, mate_normed_t = lax.optimization_barrier((d_attn, mate_normed_t))
    own, send = backward(table, saved_qkv, d_attn, attended, attended_t, weights)
    first, second = weight_parts(
        table, normed_t, mate_normed_t, incoming_t, mate_incoming_t, own, to_mate(send)
    )
    second, qkv_w = lax.optimization_barrier(([second[k] for k in range(AXES["x"])], qkv_w))
    layer_grad = norm_back(
        table, layer_input, incoming, norm_gain, own, send, qkv_w, to_mate(qkv_w)
    )
    first = exchanged(first, "y")
    second = sent_by_distance(second, "x")
    first, second, layer_grad = lax.optimization_barrier((first, second, layer_grad))
    second = added(second).astype(bf16)
    first, second = lax.optimization_barrier((first, second))
    second = exchanged(second, "y")
    first = by_distance(jnp.sum(first.astype(f32), axis=0).astype(bf16), "x")
    first = sent_by_distance(first, "x")
    second = jnp.sum(second.astype(f32), axis=0)
    first, second = lax.optimization_barrier((first, second))
    first = added(first)
    columns = jnp.concatenate([unpacked(first), unpacked(second)], axis=1).astype(bf16)
    by_z = exchanged(columns.reshape(8, 40, 320), "z")
    share = jnp.sum(by_z.astype(f32), axis=0) / (AXES["y"] * AXES["z"] * sections)
    shares = gathered(gathered(share, "x"), "core")

    def assemble(core, first_column):
        mine = [shares[core, x][:, first_column : first_column + 160] for x in range(4)]
        return [part[:, :128] for part in mine] + [part[:, 128:] for part in mine]

    qkv_weight_grad = jnp.concatenate(assemble(0, 160) + assemble(1, 160) + assemble(0, 0), axis=1)
    out_weight_grad = jnp.concatenate(assemble(1, 0), axis=1)
    return layer_grad, qkv_weight_grad, out_weight_grad


def solution(mesh):
    fine = Mesh(mesh.devices.reshape(tuple(AXES.values())), tuple(AXES))
    rows = P(("y", "z", "x", "core"), None)
    dp = P(("y", "z"), None)
    return jax.shard_map(
        on_device,
        mesh=fine,
        in_specs=(rows, rows, rows, dp, dp, P(), P(), dp, dp),
        out_specs=(rows, dp, dp),
        check_vma=False,
    )
```

```python
import functools
import math

import jax
import jax.numpy as jnp
from jax import lax
from jax.experimental import pallas as pl
from jax.experimental.pallas import tpu as pltpu
from jax.sharding import Mesh, PartitionSpec as P

HEADS = 8
HEAD_DIM = 80
TILE = 128
WINDOW = 2 * TILE
HW = HEADS * HEAD_DIM
SCALE = 1.0 / math.sqrt(HEAD_DIM)
BLOCKS = 4
QKV_PART = 1024
AXES = {"y": 4, "z": 8, "x": 4, "core": 2}
VMEM_LIMIT = 60 * 1024 * 1024

norm_eps = 1e-06
f32 = jnp.float32
bf16 = jnp.bfloat16

SOURCE, START, JOINED, META = 0, 8, 16, 24


def lane_window(head):
    first, last = head * HEAD_DIM, (head + 1) * HEAD_DIM
    return first // 128 * 128, -(-last // 128) * 128


def params():
    return pltpu.CompilerParams(vmem_limit_bytes=VMEM_LIMIT)


def cost(flops, moved):
    return pl.CostEstimate(flops=flops, bytes_accessed=moved, transcendentals=0)


def route_kernel(
    patches, owners, place, rows, table, outgoing, used, segment, own_owner, sems, *, own_tiles, src_tiles
):
    me = place[0]
    for j in range(8):
        used[j] = 0
        segment[j] = -1
        table[SOURCE + j] = -1
    for j in range(src_tiles):
        own_owner[j] = 0

    def image(i, begin):
        count = patches[0, i] // TILE
        owner = owners[0, i]
        slot = used[owner]
        used[owner] = slot + count
        for t in range(2):

            @pl.when(t < count)
            def _():
                position = begin + t
                source = position // src_tiles

                @pl.when(owner == me)
                def _():
                    table[SOURCE + slot + t] = source
                    segment[slot + t] = i

                @pl.when(source == me)
                def _():
                    own_owner[position % src_tiles] = owner

        return begin + count

    lax.fori_loop(0, patches.shape[1], image, jnp.int32(0))
    copies = []
    for j in range(src_tiles):
        first_row = pl.multiple_of(own_owner[j] * TILE, TILE)
        copy = pltpu.make_async_copy(
            rows.at[pl.ds(j * TILE, TILE)], outgoing.at[pl.ds(first_row, TILE)], sems.at[j]
        )
        copy.start()
        copies.append(copy)

    last = own_tiles - 1
    for b in range(8):
        table[START + b] = 0
        table[JOINED + b] = 0
        table[META + b] = 0
    table[META + 1] = place[1]
    table[META + 3] = place[2]
    table[META + 4] = place[3]

    def step(at):
        here = segment[at]
        after = segment[jnp.minimum(at + 1, last)]
        beyond = segment[jnp.minimum(at + 2, last)]
        joined = here == after
        splits = (at + 2 <= last) & (after == beyond) & jnp.logical_not(joined)
        return at + jnp.where(splits, 1, 2), joined

    def find(_, carry):
        at, lone = carry
        moved, _ = step(jnp.minimum(at, last))
        return jnp.where(at <= last, moved, at), lone | (at == last).astype(jnp.int32)

    _, lone = lax.fori_loop(0, BLOCKS, find, (jnp.int32(0), jnp.int32(0)))

    @pl.when(lone == 1)
    def _():
        table[START] = last - 1
        table[JOINED] = (segment[last - 1] == segment[last]).astype(jnp.int32)

    def block(_, carry):
        at, count = carry
        moved, joined = step(jnp.minimum(at, last))
        active = at < last

        @pl.when(active)
        def _():
            table[START + count] = at
            table[JOINED + count] = joined.astype(jnp.int32)

        return jnp.where(active, moved, at), count + active.astype(jnp.int32)

    _, count = lax.fori_loop(0, BLOCKS, block, (jnp.int32(0), lone))
    table[META] = count
    for copy in copies:
        copy.wait()


def route(patches, owners, place, rows, own_tiles, sections):
    src_tiles = rows.shape[0] // TILE
    smem = pl.BlockSpec(memory_space=pltpu.SMEM)
    hbm = pl.BlockSpec(memory_space=pl.ANY)
    return pl.pallas_call(
        functools.partial(route_kernel, own_tiles=own_tiles, src_tiles=src_tiles),
        out_shape=(
            jax.ShapeDtypeStruct((32,), jnp.int32),
            jax.ShapeDtypeStruct((sections * TILE, rows.shape[1]), bf16),
        ),
        in_specs=[smem, smem, smem, pl.BlockSpec(memory_space=pltpu.VMEM)],
        out_specs=(smem, hbm),
        scratch_shapes=[
            pltpu.SMEM((8,), jnp.int32),
            pltpu.SMEM((8,), jnp.int32),
            pltpu.SMEM((src_tiles,), jnp.int32),
            pltpu.SemaphoreType.DMA((src_tiles,)),
        ],
        compiler_params=params(),
        cost_estimate=cost(0, 4 * rows.size),
        name="route",
    )(patches, owners, place, rows)


def norm_kernel(x, gain, bias, out):
    wide = x[...].astype(f32)
    average = jnp.mean(wide, axis=1, keepdims=True)
    centered = wide - average
    inv_scale = lax.rsqrt(jnp.mean(centered * centered, axis=1, keepdims=True) + norm_eps)
    normed = centered * inv_scale * gain[...] + bias[...]
    out[...] = jnp.transpose(normed.astype(bf16))


def norm_transposed(x, gain, bias):
    rows, width = x.shape
    return pl.pallas_call(
        norm_kernel,
        grid=(rows // TILE,),
        out_shape=jax.ShapeDtypeStruct((width, rows), bf16),
        in_specs=[
            pl.BlockSpec((TILE, width), lambda t: (t, 0)),
            pl.BlockSpec((1, width), lambda t: (0, 0)),
            pl.BlockSpec((1, width), lambda t: (0, 0)),
        ],
        out_specs=pl.BlockSpec((width, TILE), lambda t: (0, t)),
        compiler_params=params(),
        cost_estimate=cost(10**6, 10**5),
        name="norm",
    )(x, gain.reshape(1, width), bias.reshape(1, width))


def padded_rows(values, head):
    low, high = lane_window(head)
    first = head * HEAD_DIM
    parts = []
    if first > low:
        parts.append(jnp.zeros((first - low, values.shape[1]), values.dtype))
    parts.append(values[first : first + HEAD_DIM])
    if high > first + HEAD_DIM:
        parts.append(jnp.zeros((high - first - HEAD_DIM, values.shape[1]), values.dtype))
    return jnp.concatenate(parts, axis=0) if len(parts) > 1 else parts[0]


def lane_mask(head):
    low, high = lane_window(head)
    lanes = lax.broadcasted_iota(jnp.int32, (1, high - low), 1) + low
    return ((lanes >= head * HEAD_DIM) & (lanes < (head + 1) * HEAD_DIM)).astype(f32).astype(bf16)


def matmul(a, b):
    return lax.dot_general(a, b, (((1,), (0,)), ((), ())), preferred_element_type=f32)


def block_at(rank):
    return lambda b, t: (jnp.minimum(b, jnp.maximum(t[META] - 1, 0)),) + (0,) * (rank - 1)


def softmax_over_rows(scores):
    scores = scores * (SCALE * math.log2(math.e))
    shifted = jnp.exp2(scores - jnp.max(scores, axis=0, keepdims=True))
    return (shifted * (1.0 / jnp.sum(shifted, axis=0, keepdims=True))).astype(bf16)


def forward_kernel(table, qkv, attended, attended_t, weights):
    b = pl.program_id(0)
    rows = pl.ds(pl.multiple_of(table[START + b] * TILE, TILE), WINDOW)
    joined = table[JOINED + b] == 1

    def attend(whole_window):
        queries_t = jnp.transpose(qkv[rows, 0:HW])
        values_t = jnp.transpose(qkv[rows, 2 * HW : 3 * HW])

        def scores_of(h):
            low, high = lane_window(h)
            return matmul(qkv[rows, HW + low : HW + high], padded_rows(queries_t, h))

        heads = []
        for h in range(HEADS):
            scores = scores_of(h)
            if whole_window:
                kept = softmax_over_rows(scores)
            else:
                nothing = jnp.zeros((TILE, TILE), bf16)
                top = softmax_over_rows(scores[:TILE, :TILE])
                bottom = softmax_over_rows(scores[TILE:, TILE:])
                kept = jnp.concatenate(
                    [
                        jnp.concatenate([top, nothing], axis=1),
                        jnp.concatenate([nothing, bottom], axis=1),
                    ],
                    axis=0,
                )
            weights[0, h] = kept
            heads.append(matmul(values_t[h * HEAD_DIM : (h + 1) * HEAD_DIM], kept).astype(bf16))
        whole = jnp.concatenate(heads, axis=0)
        attended_t[0] = whole
        attended[rows, :] = jnp.transpose(whole)

    pl.when((b < table[META]) & joined)(lambda: attend(True))
    pl.when((b < table[META]) & jnp.logical_not(joined))(lambda: attend(False))


def forward(table, qkv):
    rows, width = qkv.shape
    return pl.pallas_call(
        forward_kernel,
        grid_spec=pltpu.PrefetchScalarGridSpec(
            num_scalar_prefetch=1,
            grid=(BLOCKS,),
            in_specs=[pl.BlockSpec((rows, width), lambda b, t: (0, 0))],
            out_specs=(
                pl.BlockSpec((rows, HW), lambda b, t: (0, 0)),
                pl.BlockSpec((1, HW, WINDOW), block_at(3)),
                pl.BlockSpec((1, HEADS, WINDOW, WINDOW), block_at(4)),
            ),
        ),
        out_shape=(
            jax.ShapeDtypeStruct((rows, HW), bf16),
            jax.ShapeDtypeStruct((BLOCKS, HW, WINDOW), bf16),
            jax.ShapeDtypeStruct((BLOCKS, HEADS, WINDOW, WINDOW), bf16),
        ),
        compiler_params=params(),
        cost_estimate=cost(10**6, 10**5),
        name="attend",
    )(table, qkv)


def incoming_kernel(
    table, arrived, spread, qkv_in, incoming, d_attn, incoming_t, qkv_out, landing, w, sems, *, tiles
):
    t = pl.program_id(0)
    places = AXES["y"]
    piece = spread.shape[0]

    def w_copy(k):
        row = pl.multiple_of(lax.rem(table[META + 4] - k + places, places) * piece, piece)
        return pltpu.make_async_copy(
            spread.at[:, pl.ds(QKV_PART + k * HW, HW)], w.at[pl.ds(row, piece)], sems.at[tiles + k]
        )

    def row_copy(j, source):
        first_row = pl.multiple_of(source * TILE, TILE)
        return pltpu.make_async_copy(
            arrived.at[pl.ds(first_row, TILE)], landing.at[pl.ds(j * TILE, TILE)], sems.at[j]
        )

    @pl.when(t == 0)
    def _():
        for y in range(places):
            w_copy(y).start()
        for j in range(tiles):
            source = table[SOURCE + j]

            @pl.when(source >= 0)
            def _():
                row_copy(j, source).start()

            @pl.when(source < 0)
            def _():
                landing[j * TILE : (j + 1) * TILE] = jnp.zeros((TILE, landing.shape[1]), bf16)

    for i in range(2):
        j = 2 * t + i
        pl.when(table[SOURCE + j] >= 0)(row_copy(j, 0).wait)
    rows = landing[pl.ds(pl.multiple_of(t * WINDOW, WINDOW), WINDOW)]
    incoming[...] = rows
    incoming_t[...] = jnp.transpose(rows)

    @pl.when(t == 0)
    def _():
        qkv_out[...] = qkv_in[...]
        for y in range(places):
            w_copy(y).wait()

    d_attn[...] = matmul(rows, w[...]).astype(bf16)


def place_incoming(table, arrived, spread, rows):
    width = arrived.shape[1]
    qkv_part = pl.BlockSpec((spread.shape[0], QKV_PART), lambda i, t: (0, 0))
    return pl.pallas_call(
        functools.partial(incoming_kernel, tiles=rows // TILE),
        grid_spec=pltpu.PrefetchScalarGridSpec(
            num_scalar_prefetch=1,
            grid=(rows // WINDOW,),
            in_specs=[
                pl.BlockSpec(memory_space=pl.ANY),
                pl.BlockSpec(memory_space=pl.ANY),
                qkv_part,
            ],
            out_specs=(
                pl.BlockSpec((WINDOW, width), lambda i, t: (i, 0)),
                pl.BlockSpec((WINDOW, HW), lambda i, t: (i, 0)),
                pl.BlockSpec((width, WINDOW), lambda i, t: (0, i)),
                qkv_part,
            ),
            scratch_shapes=[
                pltpu.VMEM((rows, width), bf16),
                pltpu.VMEM((width, HW), bf16),
                pltpu.SemaphoreType.DMA((rows // TILE + AXES["y"],)),
            ],
        ),
        out_shape=(
            jax.ShapeDtypeStruct((rows, width), bf16),
            jax.ShapeDtypeStruct((rows, HW), bf16),
            jax.ShapeDtypeStruct((width, rows), bf16),
            jax.ShapeDtypeStruct((spread.shape[0], QKV_PART), bf16),
        ),
        compiler_params=params(),
        cost_estimate=cost(2 * rows * width * HW, 10 * rows * width),
        name="incoming",
    )(table, arrived, spread, spread)


def add_lanes(tiles, low, part):
    for j in range(part.shape[1] // 128):
        piece = part[:, j * 128 : (j + 1) * 128]
        at = low // 128 + j
        tiles[at] = piece if tiles[at] is None else tiles[at] + piece


def backward_kernel(table, qkv, d_attn, attended, attended_t, weights, own, send):
    b = pl.program_id(0)
    rows = pl.ds(pl.multiple_of(table[START + b] * TILE, TILE), WINDOW)
    joined = table[JOINED + b] == 1
    first = table[META + 1] == 0

    def grads(whole_window):
        grad_t = jnp.transpose(d_attn[rows, :])
        keys_t = jnp.transpose(qkv[rows, HW : 2 * HW])
        query_grads = []
        key_tiles = [None] * (HW // 128)
        value_tiles = [None] * (HW // 128)
        for h in range(HEADS):
            low, high = lane_window(h)
            mine = slice(h * HEAD_DIM, (h + 1) * HEAD_DIM)
            mask = lane_mask(h)
            prob_grad = matmul(qkv[rows, 2 * HW + low : 2 * HW + high], padded_rows(grad_t, h))
            row_delta = jnp.sum(
                grad_t[mine].astype(f32) * attended_t[0, mine].astype(f32), axis=0, keepdims=True
            )

            def score_grad(keys, queries):
                change = (prob_grad[keys, queries] - row_delta[:, queries]) * SCALE
                return (weights[0, h, keys, queries].astype(f32) * change).astype(bf16)

            if whole_window:
                dscore = score_grad(slice(0, WINDOW), slice(0, WINDOW))
            else:
                nothing = jnp.zeros((TILE, TILE), bf16)
                top = score_grad(slice(0, TILE), slice(0, TILE))
                bottom = score_grad(slice(TILE, WINDOW), slice(TILE, WINDOW))
                dscore = jnp.concatenate(
                    [
                        jnp.concatenate([top, nothing], axis=1),
                        jnp.concatenate([nothing, bottom], axis=1),
                    ],
                    axis=0,
                )
            query_grads.append(matmul(keys_t[mine], dscore).astype(bf16))
            add_lanes(key_tiles, low, matmul(dscore, qkv[rows, low:high] * mask))
            add_lanes(value_tiles, low, matmul(weights[0, h], d_attn[rows, low:high] * mask))

        def store(lanes, on_zero, on_one):
            own[rows, lanes] = jnp.where(first, on_zero, on_one)
            send[rows, lanes] = jnp.where(first, on_one, on_zero)

        d_query = jnp.transpose(jnp.concatenate(query_grads, axis=0))
        for j in range(HW // 128):
            lanes = slice(j * 128, (j + 1) * 128)
            store(lanes, value_tiles[j].astype(bf16), attended[rows, lanes])
            store(
                slice(HW + j * 128, HW + (j + 1) * 128), d_query[:, lanes], key_tiles[j].astype(bf16)
            )

    pl.when((b < table[META]) & joined)(lambda: grads(True))
    pl.when((b < table[META]) & jnp.logical_not(joined))(lambda: grads(False))


def backward(table, qkv, d_attn, attended, attended_t, weights):
    rows, width = qkv.shape
    whole = pl.BlockSpec((rows, HW), lambda b, t: (0, 0))
    return pl.pallas_call(
        backward_kernel,
        grid_spec=pltpu.PrefetchScalarGridSpec(
            num_scalar_prefetch=1,
            grid=(BLOCKS,),
            in_specs=[
                pl.BlockSpec((rows, width), lambda b, t: (0, 0)),
                whole,
                whole,
                pl.BlockSpec((1, HW, WINDOW), block_at(3)),
                pl.BlockSpec((1, HEADS, WINDOW, WINDOW), block_at(4)),
            ],
            out_specs=(pl.BlockSpec((rows, 2 * HW), lambda b, t: (0, 0)),) * 2,
        ),
        out_shape=(jax.ShapeDtypeStruct((rows, 2 * HW), bf16),) * 2,
        compiler_params=params(),
        cost_estimate=cost(12 * 10**9, 20 * 10**6),
        name="attend_back",
    )(table, qkv, d_attn, attended, attended_t, weights)


def norm_back_kernel(table, x, incoming, gain, own, send, own_w, mate_w, out):
    def halves(value_query, attended_key, low, high):
        grads = jnp.concatenate(
            [value_query[:, HW:], attended_key[:, HW:], value_query[:, :HW]], axis=1
        )
        contract = (((1,), (1,)), ((), ()))
        return lax.dot_general(
            grads[:, :1024], low[...], contract, preferred_element_type=f32
        ) + lax.dot_general(
            grads[:, 1024:], high[:, 128:1024], contract, preferred_element_type=f32
        )

    def finish(dnormed):
        wide = x[...].astype(f32)
        average = jnp.mean(wide, axis=1, keepdims=True)
        centered = wide - average
        inv_scale = lax.rsqrt(jnp.mean(centered * centered, axis=1, keepdims=True) + norm_eps)
        normalized = centered * inv_scale
        scaled_grad = dnormed * gain[...]
        branch = inv_scale * (
            scaled_grad
            - jnp.mean(scaled_grad, axis=1, keepdims=True)
            - normalized * jnp.mean(scaled_grad * normalized, axis=1, keepdims=True)
        )
        out[...] = (incoming[...].astype(f32) + branch).astype(bf16)

    first = table[META + 1] == 0

    @pl.when(first)
    def _():
        finish(halves(own, send, own_w, mate_w))

    @pl.when(jnp.logical_not(first))
    def _():
        finish(halves(send, own, mate_w, own_w))


def norm_back(table, x, incoming, gain, own, send, own_w, mate_w):
    rows, width = x.shape
    wide = pl.BlockSpec((WINDOW, width), lambda i, t: (i, 0))
    weights = pl.BlockSpec((width, 1024), lambda i, t: (0, 0))
    return pl.pallas_call(
        norm_back_kernel,
        grid_spec=pltpu.PrefetchScalarGridSpec(
            num_scalar_prefetch=1,
            grid=(rows // WINDOW,),
            in_specs=[
                wide,
                wide,
                pl.BlockSpec((1, width), lambda i, t: (0, 0)),
                pl.BlockSpec((WINDOW, 2 * HW), lambda i, t: (i, 0)),
                pl.BlockSpec((WINDOW, 2 * HW), lambda i, t: (i, 0)),
                weights,
                weights,
            ],
            out_specs=wide,
        ),
        out_shape=jax.ShapeDtypeStruct((rows, width), bf16),
        compiler_params=params(),
        cost_estimate=cost(2 * rows * width * 3 * HW, 20 * 10**6),
        name="norm_back",
    )(table, x, incoming, gain.reshape(1, width), own, send, own_w, mate_w)


def packed_columns(total, store):
    rows = total.shape[0]
    group = rows // 4
    fifth = total[:, 512:640]
    quarter = lax.broadcasted_iota(jnp.int32, (group, 128), 1) // 32
    for x in range(4):
        packed = jnp.zeros((group, 128), f32)
        for g in range(4):
            piece = fifth[g * group : (g + 1) * group]
            shift = (g - x) * 32 % 128
            packed = jnp.where(quarter == g, pltpu.roll(piece, shift, 1) if shift else piece, packed)
        store(x, jnp.concatenate([total[:, x * 128 : (x + 1) * 128], packed], axis=0).astype(bf16))


def weight_kernel(table, normed, mate_normed, incoming, mate_incoming, own, mate, by_y, by_x):
    first = table[META + 1] == 0
    left = jnp.where(first, normed[...], incoming[...])
    mate_left = jnp.where(first, mate_normed[...], mate_incoming[...])
    to_x = matmul(normed[...], own[:, HW:]) + matmul(mate_normed[...], mate[:, HW:])
    to_y = matmul(left, own[:, :HW]) + matmul(mate_left, mate[:, :HW])

    def store_x(x, value):
        by_x[lax.rem(x - table[META + 3] + 4, 4)] = value

    def store_y(x, value):
        by_y[x] = value

    packed_columns(to_x, store_x)
    packed_columns(to_y, store_y)


def weight_parts(table, normed, mate_normed, incoming, mate_incoming, own, mate):
    width, rows = normed.shape
    piece = width // 4
    packed = piece * 5 // 4
    left = pl.BlockSpec((piece, rows), lambda i, t: (i, 0))
    on_one = pl.BlockSpec((piece, rows), lambda i, t: (i * t[META + 1], 0))
    right = pl.BlockSpec((rows, 2 * HW), lambda i, t: (0, 0))
    return pl.pallas_call(
        weight_kernel,
        grid_spec=pltpu.PrefetchScalarGridSpec(
            num_scalar_prefetch=1,
            grid=(4,),
            in_specs=[left, left, on_one, on_one, right, right],
            out_specs=(
                pl.BlockSpec((None, 4, packed, 128), lambda i, t: (i, 0, 0, 0)),
                pl.BlockSpec((4, None, packed, 128), lambda i, t: (0, i, 0, 0)),
            ),
        ),
        out_shape=(jax.ShapeDtypeStruct((4, 4, packed, 128), bf16),) * 2,
        compiler_params=params(),
        cost_estimate=cost(8 * width * rows * HW, 8 * width * rows + 4 * width * HW),
        name="weight_parts",
    )(table, normed, mate_normed, incoming, mate_incoming, own, mate)


def unpacked(part):
    rest = part[320:]
    return jnp.concatenate(
        [part[:320], jnp.concatenate([rest[:, i * 32 : (i + 1) * 32] for i in range(4)], axis=0)], axis=1
    )


def to_mate(value):
    return lax.ppermute(value, "core", [(0, 1), (1, 0)])


def gathered(value, axis):
    count = AXES[axis]
    here = lax.axis_index(axis)
    out = jnp.zeros((count,) + value.shape, value.dtype)
    out = lax.dynamic_update_index_in_dim(out, value, here, 0)
    for k in range(1, count):
        part = lax.ppermute(value, axis, [(i, (i + k) % count) for i in range(count)])
        out = lax.dynamic_update_index_in_dim(out, part, lax.rem(here - k + count, count), 0)
    return out


def sent_by_distance(parts, axis):
    count = AXES[axis]
    return [parts[0]] + [
        lax.ppermute(parts[k], axis, [(i, (i + k) % count) for i in range(count)])
        for k in range(1, count)
    ]


def by_distance(value, axis):
    return jnp.roll(value, -lax.axis_index(axis), axis=0)


def added(parts):
    return sum(part.astype(f32) for part in parts)


def exchanged(value, axes):
    return lax.all_to_all(value, axes, split_axis=0, concat_axis=0, tiled=True)


def on_device(
    grad_rows,
    layer_input,
    saved_qkv,
    image_patches,
    image_owner,
    norm_gain,
    norm_bias,
    w_qkv,
    w_out,
):
    width = layer_input.shape[1]
    own_tiles = layer_input.shape[0] // TILE
    section = ("x", "core")
    sections = AXES["x"] * AXES["core"]
    core = lax.axis_index("core")
    place = jnp.stack([lax.axis_index(section), core, lax.axis_index("x"), lax.axis_index("y")]).astype(jnp.int32)

    spread = jnp.concatenate(
        [lax.dynamic_slice_in_dim(w_qkv, 896 * core, QKV_PART, axis=1)]
        + sent_by_distance([w_out] * AXES["y"], "y"),
        axis=1,
    )
    table, outgoing = route(image_patches, image_owner, place, grad_rows, own_tiles, sections)
    arrived = exchanged(outgoing, section)
    spread = lax.all_gather(spread, "z", axis=0, tiled=True)
    normed_t = norm_transposed(layer_input, norm_gain, norm_bias)
    mate_normed_t = to_mate(normed_t)
    attended, attended_t, weights = forward(table, saved_qkv)
    spread, arrived, attended_t, normed_t = lax.optimization_barrier(
        (spread, arrived, attended_t, normed_t)
    )
    incoming, d_attn, incoming_t, qkv_w = place_incoming(table, arrived, spread, own_tiles * TILE)
    qkv_w = lax.all_gather(qkv_w, "y", axis=0, tiled=True)
    mate_incoming_t = to_mate(incoming_t)
    d_attn, mate_normed_t = lax.optimization_barrier((d_attn, mate_normed_t))
    own, send = backward(table, saved_qkv, d_attn, attended, attended_t, weights)
    first, second = weight_parts(
        table, normed_t, mate_normed_t, incoming_t, mate_incoming_t, own, to_mate(send)
    )
    second, qkv_w = lax.optimization_barrier(([second[k] for k in range(AXES["x"])], qkv_w))
    layer_grad = norm_back(
        table, layer_input, incoming, norm_gain, own, send, qkv_w, to_mate(qkv_w)
    )
    first = exchanged(first, "y")
    second = sent_by_distance(second, "x")
    first, second, layer_grad = lax.optimization_barrier((first, second, layer_grad))
    second = added(second).astype(bf16)
    first, second = lax.optimization_barrier((first, second))
    second = exchanged(second, "y")
    first = by_distance(jnp.sum(first.astype(f32), axis=0).astype(bf16), "x")
    first = sent_by_distance(first, "x")
    second = jnp.sum(second.astype(f32), axis=0)
    first, second = lax.optimization_barrier((first, second))
    first = added(first)
    columns = jnp.concatenate([unpacked(first), unpacked(second)], axis=1).astype(bf16)
    by_z = exchanged(columns.reshape(8, 40, 320), "z")
    share = jnp.sum(by_z.astype(f32), axis=0) / (AXES["y"] * AXES["z"] * sections)
    shares = gathered(gathered(share, "x"), "core")

    def assemble(core, first_column):
        mine = [shares[core, x][:, first_column : first_column + 160] for x in range(4)]
        return [part[:, :128] for part in mine] + [part[:, 128:] for part in mine]

    qkv_weight_grad = jnp.concatenate(assemble(0, 160) + assemble(1, 160) + assemble(0, 0), axis=1)
    out_weight_grad = jnp.concatenate(assemble(1, 0), axis=1)
    return layer_grad, qkv_weight_grad, out_weight_grad


def solution(mesh):
    fine = Mesh(mesh.devices.reshape(tuple(AXES.values())), tuple(AXES))
    rows = P(("y", "z", "x", "core"), None)
    dp = P(("y", "z"), None)
    return jax.shard_map(
        on_device,
        mesh=fine,
        in_specs=(rows, rows, rows, dp, dp, P(), P(), dp, dp),
        out_specs=(rows, dp, dp),
        check_vma=False,
    )
```
